512 devices in a mesh: dp: 32 (over z, y_hi, core), group: 16 (over x, y_lo).
Axes of the slice: x: 4, y: 8 (y_hi: 2, y_lo: 4; y = y_hi * 4 + y_lo), z: 8, core: 2. Of those that a mesh axis runs over, the one named last changes fastest.
Arguments:
- features: bfloat16 [32768, 5, 2048], P(('dp', 'group')), may hold values from -24 to 24
- labels: int32 [32768], P(('dp', 'group')), may hold values from 0 to 2
- weight: float32 [2048, 384], P('group'), may hold values from -0.125 to 0.125
- head: float32 [384, 3], replicated, may hold values from -24 to 24
- moment_one: float32 [2048, 384], P('group'), may hold values from -3 to 3
- moment_two: float32 [2048, 384], P('group'), may hold values from 0.1 to 2
Outputs:
- input_grad: bfloat16 [32768, 5, 2048], P(('dp', 'group'))
- new_weight: float32 [2048, 384], P('group')
- new_first: float32 [2048, 384], P('group')
- new_second: float32 [2048, 384], P('group')
The draws below stay inside these ranges and needn't reach their ends.
All inputs are finite; a program needn't handle non-finite values.
Results may differ from the reference program's by a relative error of at most 0.012.
Values may be sent and summed in bfloat16 or wider, within the bound.
No kernel may reach another device: no remote copies, remote signals or barrier semaphores. Data moves between devices by JAX's collectives and lax.ppermute only.
A program may use at most 128 MiB of HBM per device.

```python
import math
import jax
import jax.numpy as jnp
from jax import lax

C_IN = 2048
C_OUT = 384
CLASSES = 3
POS = 5
PILE_DEV = 64
TOKENS = 32768


def draw_head(key, part):
    key = jax.random.fold_in(key, 7)
    values = jnp.clip(jax.random.normal(key, (C_OUT, CLASSES), jnp.float32), -3.0, 3.0)
    return values * 0.5


def touch_ends(entries, rng, smallest, largest):
    longest = entries.shape.index(max(entries.shape))
    spots = []
    for shift in (0, 1):
        where = [jax.random.randint(jax.random.fold_in(rng, axis), (), 0, length) for axis, length in enumerate(entries.shape)]
        where[longest] = (where[longest] + shift) % entries.shape[longest]
        spots.append(tuple(where))
    return entries.at[spots[0]].set(smallest).at[spots[1]].set(largest)


def with_spikes(entries, rng, source, target, blocks, factor):
    owner, partner = [(jnp.arange(entries.shape[position]) // (entries.shape[position] // blocks)).reshape([-1 if axis == position else 1 for axis in range(entries.ndim)]) for position in (source, target)]
    chosen = jax.random.permutation(rng, blocks)[partner]
    strong = (owner == chosen) | (owner == (partner + blocks // 2) % blocks)
    return jnp.where(strong, factor * entries, entries)


def level_of(rng, shape, cuts, low, top_value):
    level, own = 1.0, jax.random.fold_in(rng, 6)
    for axis_at, blocks in cuts:
        draws = jnp.exp(jax.random.uniform(jax.random.fold_in(own, axis_at), (blocks,), jnp.float32, low / len(cuts), top_value / len(cuts)))
        level = level * jnp.repeat(draws, shape[axis_at] // blocks).reshape([-1 if axis == axis_at else 1 for axis in range(len(shape))])
    return level


def gaussian(stream_key, extent, deviation, limit, cuts=(), kind=jnp.bfloat16):
    entries = deviation * jax.random.normal(stream_key, extent, jnp.float32)
    if cuts:
        entries = entries * level_of(stream_key, extent, cuts, -0.22, 0.18)
    return jnp.clip(entries, -limit, limit).astype(kind)


def heavy_noise(stream_key, dims, spread, reach, shards, heavy, held_as=jnp.bfloat16):
    array = spread * jax.random.normal(stream_key, dims, jnp.float32)
    if shards:
        array = array * level_of(stream_key, dims, shards, -0.22, 0.18)
    return jnp.clip(with_spikes(array, jax.random.fold_in(stream_key, 3), *heavy), -reach, reach).astype(held_as)


def setup_inputs(seed: int = 0) -> dict:
    key_of = jax.random.split(jax.random.key(seed), 7)
    features = heavy_noise(key_of[0], (TOKENS, POS, C_IN), 1.0, 24.0, ((0, 512),), (0, 2, 512, 6.0))
    labels = touch_ends(jax.random.randint(key_of[1], (TOKENS,), 0, 3), jax.random.fold_in(key_of[1], 1), 0, 2).astype(jnp.int32)
    weight = gaussian(key_of[2], (C_IN, C_OUT), C_IN ** -0.5, 0.125, ((0, 16),), jnp.float32)
    head = draw_head(jax.random.fold_in(key_of[6], 71), 0)
    moment_one = gaussian(key_of[4], (C_IN, C_OUT), 0.5, 3.0, ((0, 16),), jnp.float32)
    moment_two = jnp.clip(jnp.exp(math.log(2.0) - 2.9957323 * jax.random.uniform(key_of[5], (C_IN, C_OUT), jnp.float32) ** level_of(key_of[5], (C_IN, C_OUT), ((0, 16),), -0.2, 0.2)), 0.1, 2.0)
    return dict(features=features, labels=labels, weight=weight, head=head, moment_one=moment_one, moment_two=moment_two)


beta_one = 0.9
beta_two = 0.999
learn_rate = 0.01
epsilon = 1e-08
bias_steps = 10.0

def gelu_tanh(value):
    return jax.nn.gelu(value, approximate=True)

def adam_update(weight, grad, first, second):
    new_first = beta_one * first + (1.0 - beta_one) * grad
    new_second = beta_two * second + (1.0 - beta_two) * grad * grad
    first_hat = new_first / (1.0 - beta_one ** bias_steps)
    second_hat = new_second / (1.0 - beta_two ** bias_steps)
    new_weight = weight - learn_rate * first_hat / (jnp.sqrt(second_hat) + epsilon)
    return (new_weight, new_first, new_second)

def reference(features, labels, weight, head, moment_one, moment_two):
    low_weight = weight.astype(jnp.bfloat16)
    blocks = features.reshape(-1, PILE_DEV, POS, C_IN)
    label_blocks = labels.reshape(-1, PILE_DEV)

    def step(total, pair):
        block, marks = pair
        rows = block.reshape(PILE_DEV * POS, C_IN)
        pre = jnp.dot(rows, low_weight, preferred_element_type=jnp.float32)
        act, back = jax.vjp(gelu_tanh, pre)
        pooled = lax.optimization_barrier(jnp.sum(act.reshape(PILE_DEV, POS, C_OUT), axis=1)) / POS
        logits = jnp.dot(pooled, head, precision=lax.Precision.HIGHEST)
        prob = jax.nn.softmax(logits, axis=-1)
        dlogits = prob - jax.nn.one_hot(marks, CLASSES, dtype=jnp.float32)
        dpooled = jnp.dot(dlogits, head.T, precision=lax.Precision.HIGHEST)
        dact = jnp.broadcast_to(dpooled[:, None, :] / POS, (PILE_DEV, POS, C_OUT)).reshape(PILE_DEV * POS, C_OUT)
        dpre = back(dact)[0].astype(jnp.bfloat16)
        total = total + lax.dot_general(rows, dpre, (((0,), (0,)), ((), ())), preferred_element_type=jnp.float32)
        back_rows = lax.dot_general(dpre, low_weight, (((1,), (1,)), ((), ())), preferred_element_type=jnp.float32)
        return (total, back_rows.astype(jnp.bfloat16).reshape(PILE_DEV, POS, C_IN))
    grad, input_blocks = lax.scan(step, jnp.zeros((C_IN, C_OUT), jnp.float32), (blocks, label_blocks))
    input_grad = input_blocks.reshape(-1, POS, C_IN)
    new_weight, new_first, new_second = adam_update(weight, grad, moment_one, moment_two)
    return (input_grad, new_weight, new_first, new_second)
```

```python
import functools
import math

import jax
import jax.numpy as jnp
from jax import lax
from jax.experimental import pallas as pl
from jax.experimental.pallas import tpu as pltpu
from jax.sharding import PartitionSpec as P

beta_one = 0.9
beta_two = 0.999
learn_rate = 0.01
epsilon = 1e-08
bias_steps = 10.0

AXES = ("dp", "group")
Z, YH, CORE, X, YL = 8, 2, 2, 4, 4
GROUP = X * YL
root = math.sqrt(2.0 / math.pi)
cubic = 0.044715


def index(z, yh, c, x, yl):
    return ((z * YH + yh) * CORE + c) * GROUP + x * YL + yl


def places():
    for z in range(Z):
        for yh in range(YH):
            for c in range(CORE):
                for x in range(X):
                    for yl in range(YL):
                        yield z, yh, c, x, yl


def groups(key):
    held = {}
    for place in places():
        held.setdefault(key(*place), []).append(index(*place))
    return [held[name] for name in sorted(held)]


OVER_GROUP = groups(lambda z, yh, c, x, yl: (z, yh, c))
OVER_X = groups(lambda z, yh, c, x, yl: (z, yh, c, yl))
OVER_Y = groups(lambda z, yh, c, x, yl: (z, c, x))
OVER_Z = groups(lambda z, yh, c, x, yl: (yh, c, x, yl))
SWAP = [(index(z, yh, c, x, yl), index(z, yh, 1 - c, x, yl)) for z, yh, c, x, yl in places()]


def swap_cores(value):
    return lax.ppermute(value, AXES, SWAP)


def exchange(value, members):
    return lax.all_to_all(value, AXES, 0, 0, tiled=True, axis_index_groups=members)


def join_halves(core, own_ref, other_ref, out_ref, rows):
    own_at = core * rows
    other_at = rows - own_at
    for block in range(own_ref.shape[0] // rows):
        span = pl.ds(block * rows, rows)
        base = 2 * rows * block
        out_ref[pl.ds(pl.multiple_of(base + own_at, rows), rows), :] = own_ref[span, :]
        out_ref[pl.ds(pl.multiple_of(base + other_at, rows), rows), :] = other_ref[span, :]


def core_index():
    return lax.rem(lax.axis_index("dp"), CORE)


def forward_kernel(
    own_ref, other_ref, rows_ref, labels_ref, head_ref, dpre_ref, keep_ref, send_ref, weight_ref, flip_ref
):
    core = core_index()
    positions, piles, channels = rows_ref.shape
    outputs = head_ref.shape[1]
    classes = head_ref.shape[0]
    count = positions * piles
    join_halves(core, own_ref, other_ref, weight_ref, own_ref.shape[0] // GROUP)
    rows = rows_ref[...].reshape(count, channels)
    pre = jnp.dot(rows, weight_ref[...], preferred_element_type=jnp.float32)
    square = pre * pre
    bend = jnp.tanh(root * (pre + cubic * (pre * square)))
    act = 0.5 * pre * (1.0 + bend)
    slope = 0.5 * (1.0 + bend) + 0.5 * pre * (1.0 - bend * bend) * (root * (1.0 + 3.0 * cubic * square))
    pooled = act[:piles]
    for position in range(1, positions):
        pooled = pooled + act[position * piles : (position + 1) * piles]
    pooled = pooled / positions
    heads = [head_ref[kind : kind + 1, :] for kind in range(classes)]
    logits = [jnp.sum(pooled * vector, axis=1, keepdims=True) for vector in heads]
    top = functools.reduce(jnp.maximum, logits)
    powers = [jnp.exp(value - top) for value in logits]
    total = functools.reduce(jnp.add, powers)
    across = lax.broadcasted_iota(jnp.int32, (piles, piles), 0) == lax.broadcasted_iota(
        jnp.int32, (piles, piles), 1
    )
    marks = jnp.sum(
        jnp.where(across, labels_ref[...].astype(jnp.float32), 0.0), axis=1, keepdims=True
    )
    dpooled = jnp.zeros((piles, outputs), jnp.float32)
    for kind in range(classes):
        dlogit = powers[kind] / total - jnp.where(marks == float(kind), 1.0, 0.0)
        dpooled = dpooled + dlogit * heads[kind]
    dact = dpooled / positions
    dpre = jnp.concatenate([dact] * positions, axis=0) * slope
    dpre_ref[...] = dpre.astype(jnp.bfloat16)
    flip_ref[...] = dpre.T.astype(jnp.bfloat16)
    half = outputs // 2
    keep_ref[...] = flip_ref[pl.ds(pl.multiple_of(core * half, half), half), :]
    other = flip_ref[pl.ds(pl.multiple_of((1 - core) * half, half), half), :]
    width = channels // GROUP
    for block in range(GROUP // 4):
        part = jnp.dot(
            other,
            rows_ref[:, :, 4 * width * block : 4 * width * (block + 1)].reshape(count, 4 * width),
            preferred_element_type=jnp.float32,
        ).astype(jnp.bfloat16)
        for at in range(4):
            send_ref[4 * block + at] = part[:, at * width : (at + 1) * width]


def backward_kernel(own_ref, other_ref, rows_ref, dpre_ref, keep_ref, input_ref, grad_ref, weight_ref):
    core = core_index()
    positions, piles, wide = rows_ref.shape
    join_halves(core, own_ref, other_ref, weight_ref, own_ref.shape[0] // 4)
    back = lax.dot_general(
        dpre_ref[...], weight_ref[...], (((1,), (1,)), ((), ())), preferred_element_type=jnp.float32
    )
    input_ref[...] = back.astype(jnp.bfloat16).reshape(positions, piles, wide)
    part = jnp.dot(
        keep_ref[...], rows_ref[...].reshape(positions * piles, wide), preferred_element_type=jnp.float32
    )
    width = wide // 4
    for at in range(4):
        grad_ref[at] = part[:, at * width : (at + 1) * width]


def adam_kernel(
    own_ref, other_ref, weight_ref, first_ref, second_ref, out_weight, out_first, out_second, flip_ref
):
    core = core_index()
    join_halves(core, own_ref, other_ref, flip_ref, own_ref.shape[0])
    grad = flip_ref[...].T
    new_first = beta_one * first_ref[...] + (1.0 - beta_one) * grad
    new_second = beta_two * second_ref[...] + (1.0 - beta_two) * grad * grad
    first_hat = new_first / (1.0 - beta_one**bias_steps)
    second_hat = new_second / (1.0 - beta_two**bias_steps)
    out_weight[...] = weight_ref[...] - learn_rate * first_hat / (jnp.sqrt(second_hat) + epsilon)
    out_first[...] = new_first
    out_second[...] = new_second


def per_device(features, labels, weight, head, moment_one, moment_two):
    piles, positions, channels = features.shape
    shard, outputs = weight.shape
    count = piles * positions
    half_rows = shard // 2
    half_outs = outputs // 2
    core = lax.rem(lax.axis_index("dp"), CORE)
    rows = features.transpose(1, 0, 2)

    half = lax.dynamic_slice_in_dim(weight, core * half_rows, half_rows, 0).astype(jnp.bfloat16)
    copies = jnp.broadcast_to(half[None], (GROUP, half_rows, outputs)).reshape(-1, outputs)
    own = exchange(copies, OVER_GROUP)
    other = swap_cores(own)

    vmem = pl.BlockSpec(memory_space=pltpu.VMEM)
    dpre, keep, send = pl.pallas_call(
        forward_kernel,
        out_shape=(
            jax.ShapeDtypeStruct((count, outputs), jnp.bfloat16),
            jax.ShapeDtypeStruct((half_outs, count), jnp.bfloat16),
            jax.ShapeDtypeStruct((GROUP, half_outs, shard), jnp.bfloat16),
        ),
        in_specs=[vmem] * 5,
        out_specs=(vmem, vmem, vmem),
        scratch_shapes=[
            pltpu.VMEM((channels, outputs), jnp.bfloat16),
            pltpu.VMEM((outputs, count), jnp.bfloat16),
        ],
        compiler_params=pltpu.CompilerParams(vmem_limit_bytes=32 << 20),
        cost_estimate=pl.CostEstimate(
            flops=3 * count * channels * outputs, bytes_accessed=4 << 20, transcendentals=count * outputs
        ),
        name="forward",
    )(own, other, rows, labels.reshape(1, piles), head.T)

    received = swap_cores(send)
    wide = 4 * shard
    input_grad, grad = pl.pallas_call(
        backward_kernel,
        grid=(channels // wide,),
        out_shape=(
            jax.ShapeDtypeStruct((positions, piles, channels), jnp.bfloat16),
            jax.ShapeDtypeStruct((GROUP, half_outs, shard), jnp.float32),
        ),
        in_specs=[
            pl.BlockSpec((4 * half_rows, outputs), lambda step: (step, 0)),
            pl.BlockSpec((4 * half_rows, outputs), lambda step: (step, 0)),
            pl.BlockSpec((positions, piles, wide), lambda step: (0, 0, step)),
            pl.BlockSpec((count, outputs), lambda step: (0, 0)),
            pl.BlockSpec((half_outs, count), lambda step: (0, 0)),
        ],
        out_specs=(
            pl.BlockSpec((positions, piles, wide), lambda step: (0, 0, step)),
            pl.BlockSpec((4, half_outs, shard), lambda step: (step, 0, 0)),
        ),
        scratch_shapes=[pltpu.VMEM((wide, outputs), jnp.bfloat16)],
        compiler_params=pltpu.CompilerParams(vmem_limit_bytes=32 << 20),
        cost_estimate=pl.CostEstimate(
            flops=3 * count * channels * outputs, bytes_accessed=6 << 20, transcendentals=0
        ),
        name="backward",
    )(own, other, rows, dpre, keep)

    def total(parts, members):
        return jnp.sum(parts.reshape(members, -1, half_outs, shard).astype(jnp.float32), axis=0)

    both = (grad + received.astype(jnp.float32)).astype(jnp.bfloat16)
    over_x = total(exchange(both, OVER_X), X).astype(jnp.bfloat16)
    over_y = total(exchange(jnp.concatenate([over_x] * YH, axis=0), OVER_Y), Z).astype(jnp.bfloat16)
    copies = jnp.broadcast_to(over_y, (Z, half_outs, shard))
    mine = total(exchange(copies, OVER_Z), Z)[0]
    theirs = swap_cores(mine)

    new_weight, new_first, new_second = pl.pallas_call(
        adam_kernel,
        out_shape=(jax.ShapeDtypeStruct((shard, outputs), jnp.float32),) * 3,
        in_specs=[vmem] * 5,
        out_specs=(vmem,) * 3,
        scratch_shapes=[pltpu.VMEM((outputs, shard), jnp.float32)],
        name="adam",
    )(mine, theirs, weight, moment_one, moment_two)
    return (input_grad.transpose(1, 0, 2), new_weight, new_first, new_second)


def solution(mesh):
    return jax.shard_map(
        per_device,
        mesh=mesh,
        in_specs=(
            P(("dp", "group"), None, None),
            P(("dp", "group")),
            P("group", None),
            P(),
            P("group", None),
            P("group", None),
        ),
        out_specs=(
            P(("dp", "group"), None, None),
            P("group", None),
            P("group", None),
            P("group", None),
        ),
        check_vma=False,
    )
```

```python
import functools
import math

import jax
import jax.numpy as jnp
from jax import lax
from jax.experimental import pallas as pl
from jax.experimental.pallas import tpu as pltpu
from jax.sharding import PartitionSpec as P

beta_one = 0.9
beta_two = 0.999
learn_rate = 0.01
epsilon = 1e-08
bias_steps = 10.0

AXES = ("dp", "group")
Z, YH, CORE, X, YL = 8, 2, 2, 4, 4
Y = YH * YL
GROUP = X * YL
root = math.sqrt(2.0 / math.pi)
cubic = 0.044715


def index(z, yh, c, x, yl):
    return ((z * YH + yh) * CORE + c) * GROUP + x * YL + yl


def places():
    for z in range(Z):
        for yh in range(YH):
            for c in range(CORE):
                for x in range(X):
                    for yl in range(YL):
                        yield z, yh, c, x, yl


def groups(key, order):
    held = {}
    for place in places():
        held.setdefault(key(*place), []).append((order(*place), index(*place)))
    return [[at for _, at in sorted(held[name])] for name in sorted(held)]


def line(yh, yl, c):
    return (yh * YL + yl + (Y - 2 * c)) % Y // YL


OVER_GROUP = groups(lambda z, yh, c, x, yl: (z, c, line(yh, yl, c)), lambda z, yh, c, x, yl: (x, yl))
OVER_Z = groups(lambda z, yh, c, x, yl: (yh, c, x, yl), lambda z, yh, c, x, yl: z)
OVER_REST = groups(lambda z, yh, c, x, yl: (z, x, yl), lambda z, yh, c, x, yl: (yh, c))
SWAP = [(index(z, yh, c, x, yl), index(z, yh, 1 - c, x, yl)) for z, yh, c, x, yl in places()]


def swap_cores(value):
    return lax.ppermute(value, AXES, SWAP)


def exchange(value, members):
    return lax.all_to_all(value, AXES, 0, 0, tiled=True, axis_index_groups=members)


def join_halves(core, own_ref, other_ref, out_ref, rows):
    own_at = core * rows
    other_at = rows - own_at
    for block in range(own_ref.shape[0] // rows):
        span = pl.ds(block * rows, rows)
        base = 2 * rows * block
        out_ref[pl.ds(pl.multiple_of(base + own_at, rows), rows), :] = own_ref[span, :]
        out_ref[pl.ds(pl.multiple_of(base + other_at, rows), rows), :] = other_ref[span, :]


def core_index():
    return lax.rem(lax.axis_index("dp"), CORE)


def forward_kernel(
    _, own_ref, other_ref, rows_ref, labels_ref, head_ref, dpre_ref, keep_ref, send_ref, weight_ref, flip_ref
):
    core = core_index()
    positions, piles, channels = rows_ref.shape
    outputs = head_ref.shape[1]
    classes = head_ref.shape[0]
    count = positions * piles
    join_halves(core, own_ref, other_ref, weight_ref, own_ref.shape[0] // GROUP)
    rows = rows_ref[...].reshape(count, channels)
    pre = jnp.dot(rows, weight_ref[...], preferred_element_type=jnp.float32)
    square = pre * pre
    bend = jnp.tanh(root * (pre + cubic * (pre * square)))
    act = 0.5 * pre * (1.0 + bend)
    slope = 0.5 * (1.0 + bend) + 0.5 * pre * (1.0 - bend * bend) * (root * (1.0 + 3.0 * cubic * square))
    pooled = act[:piles]
    for position in range(1, positions):
        pooled = pooled + act[position * piles : (position + 1) * piles]
    pooled = pooled / positions
    heads = [head_ref[kind : kind + 1, :] for kind in range(classes)]
    logits = [jnp.sum(pooled * vector, axis=1, keepdims=True) for vector in heads]
    top = functools.reduce(jnp.maximum, logits)
    powers = [jnp.exp(value - top) for value in logits]
    total = functools.reduce(jnp.add, powers)
    across = lax.broadcasted_iota(jnp.int32, (piles, piles), 0) == lax.broadcasted_iota(
        jnp.int32, (piles, piles), 1
    )
    marks = jnp.sum(
        jnp.where(across, labels_ref[...].astype(jnp.float32), 0.0), axis=1, keepdims=True
    )
    dpooled = jnp.zeros((piles, outputs), jnp.float32)
    for kind in range(classes):
        dlogit = powers[kind] / total - jnp.where(marks == float(kind), 1.0, 0.0)
        dpooled = dpooled + dlogit * heads[kind]
    dact = dpooled / positions
    dpre = jnp.concatenate([dact] * positions, axis=0) * slope
    dpre_ref[...] = dpre.astype(jnp.bfloat16)
    flip_ref[...] = dpre.T.astype(jnp.bfloat16)
    half = outputs // 2
    keep_ref[...] = flip_ref[pl.ds(pl.multiple_of(core * half, half), half), :]
    other = flip_ref[pl.ds(pl.multiple_of((1 - core) * half, half), half), :]
    width = channels // GROUP
    for block in range(GROUP // 4):
        part = jnp.dot(
            other,
            rows_ref[:, :, 4 * width * block : 4 * width * (block + 1)].reshape(count, 4 * width),
            preferred_element_type=jnp.float32,
        ).astype(jnp.bfloat16)
        for at in range(4):
            send_ref[4 * block + at] = part[:, at * width : (at + 1) * width]


def backward_kernel(own_ref, other_ref, rows_ref, dpre_ref, keep_ref, input_ref, grad_ref, weight_ref):
    core = core_index()
    positions, piles, wide = rows_ref.shape
    join_halves(core, own_ref, other_ref, weight_ref, own_ref.shape[0] // 4)
    back = lax.dot_general(
        dpre_ref[...], weight_ref[...], (((1,), (1,)), ((), ())), preferred_element_type=jnp.float32
    )
    input_ref[...] = back.astype(jnp.bfloat16).reshape(positions, piles, wide)
    part = jnp.dot(
        keep_ref[...], rows_ref[...].reshape(positions * piles, wide), preferred_element_type=jnp.float32
    )
    width = wide // 4
    for at in range(4):
        grad_ref[at] = part[:, at * width : (at + 1) * width]


def stage_kernel(_, weight_ref, first_ref, second_ref, out_weight, out_first, out_second):
    out_weight[...] = weight_ref[...]
    out_first[...] = first_ref[...]
    out_second[...] = second_ref[...]


def adam_kernel(parts_ref, weight_ref, first_ref, second_ref, out_weight, out_first, out_second):
    parts = [parts_ref[at].astype(jnp.float32) for at in range(YH * CORE)]
    halves = [functools.reduce(jnp.add, parts[core::CORE]) for core in range(CORE)]
    grad = jnp.concatenate(halves, axis=0).T
    new_first = beta_one * first_ref[...] + (1.0 - beta_one) * grad
    new_second = beta_two * second_ref[...] + (1.0 - beta_two) * grad * grad
    first_hat = new_first / (1.0 - beta_one**bias_steps)
    second_hat = new_second / (1.0 - beta_two**bias_steps)
    out_weight[...] = weight_ref[...] - learn_rate * first_hat / (jnp.sqrt(second_hat) + epsilon)
    out_first[...] = new_first
    out_second[...] = new_second


def per_device(features, labels, weight, head, moment_one, moment_two):
    piles, positions, channels = features.shape
    shard, outputs = weight.shape
    count = piles * positions
    half_rows = shard // 2
    half_outs = outputs // 2
    core = lax.rem(lax.axis_index("dp"), CORE)
    rows = features.transpose(1, 0, 2)

    half = lax.dynamic_slice_in_dim(weight, core * half_rows, half_rows, 0).astype(jnp.bfloat16)
    copies = jnp.broadcast_to(half[None], (GROUP, half_rows, outputs)).reshape(-1, outputs)
    own = exchange(copies, OVER_GROUP)
    other = swap_cores(own)

    vmem = pl.BlockSpec(memory_space=pltpu.VMEM)
    anywhere = pl.BlockSpec(memory_space=pl.ANY)
    staged = pl.pallas_call(
        stage_kernel,
        out_shape=(jax.ShapeDtypeStruct((shard, outputs), jnp.float32),) * 3,
        in_specs=[anywhere] + [vmem] * 3,
        out_specs=(vmem,) * 3,
        cost_estimate=pl.CostEstimate(flops=0, bytes_accessed=2 << 20, transcendentals=0),
        name="stage",
    )(own, weight, moment_one, moment_two)
    dpre, keep, send = pl.pallas_call(
        forward_kernel,
        out_shape=(
            jax.ShapeDtypeStruct((count, outputs), jnp.bfloat16),
            jax.ShapeDtypeStruct((half_outs, count), jnp.bfloat16),
            jax.ShapeDtypeStruct((GROUP, half_outs, shard), jnp.bfloat16),
        ),
        in_specs=[anywhere] + [vmem] * 5,
        out_specs=(vmem, vmem, vmem),
        scratch_shapes=[
            pltpu.VMEM((channels, outputs), jnp.bfloat16),
            pltpu.VMEM((outputs, count), jnp.bfloat16),
        ],
        compiler_params=pltpu.CompilerParams(vmem_limit_bytes=32 << 20),
        cost_estimate=pl.CostEstimate(
            flops=3 * count * channels * outputs, bytes_accessed=4 << 20, transcendentals=count * outputs
        ),
        name="forward",
    )(staged[0], own, other, rows, labels.reshape(1, piles), head.T)

    received = swap_cores(send)
    wide = 4 * shard
    input_grad, grad = pl.pallas_call(
        backward_kernel,
        grid=(channels // wide,),
        out_shape=(
            jax.ShapeDtypeStruct((positions, piles, channels), jnp.bfloat16),
            jax.ShapeDtypeStruct((GROUP, half_outs, shard), jnp.float32),
        ),
        in_specs=[
            pl.BlockSpec((4 * half_rows, outputs), lambda step: (step, 0)),
            pl.BlockSpec((4 * half_rows, outputs), lambda step: (step, 0)),
            pl.BlockSpec((positions, piles, wide), lambda step: (0, 0, step)),
            pl.BlockSpec((count, outputs), lambda step: (0, 0)),
            pl.BlockSpec((half_outs, count), lambda step: (0, 0)),
        ],
        out_specs=(
            pl.BlockSpec((positions, piles, wide), lambda step: (0, 0, step)),
            pl.BlockSpec((4, half_outs, shard), lambda step: (step, 0, 0)),
        ),
        scratch_shapes=[pltpu.VMEM((wide, outputs), jnp.bfloat16)],
        compiler_params=pltpu.CompilerParams(vmem_limit_bytes=32 << 20),
        cost_estimate=pl.CostEstimate(
            flops=3 * count * channels * outputs, bytes_accessed=6 << 20, transcendentals=0
        ),
        name="backward",
    )(own, other, rows, dpre, keep)

    def total(parts, members):
        return jnp.sum(parts.reshape(members, -1, half_outs, shard).astype(jnp.float32), axis=0)

    both = (grad + received.astype(jnp.float32)).astype(jnp.bfloat16)
    over_group = total(exchange(both, OVER_GROUP), GROUP).astype(jnp.bfloat16)
    copies = jnp.broadcast_to(over_group, (Z, half_outs, shard))
    over_z = total(exchange(copies, OVER_Z), Z).astype(jnp.bfloat16)
    copies = jnp.broadcast_to(over_z, (YH * CORE, half_outs, shard))
    parts = exchange(copies, OVER_REST)

    new_weight, new_first, new_second = pl.pallas_call(
        adam_kernel,
        out_shape=(jax.ShapeDtypeStruct((shard, outputs), jnp.float32),) * 3,
        in_specs=[vmem] * 4,
        out_specs=(vmem,) * 3,
        name="adam",
    )(parts, *staged)
    return (input_grad.transpose(1, 0, 2), new_weight, new_first, new_second)


def solution(mesh):
    return jax.shard_map(
        per_device,
        mesh=mesh,
        in_specs=(
            P(("dp", "group"), None, None),
            P(("dp", "group")),
            P("group", None),
            P(),
            P("group", None),
            P("group", None),
        ),
        out_specs=(
            P(("dp", "group"), None, None),
            P("group", None),
            P("group", None),
            P("group", None),
        ),
        check_vma=False,
    )
```

```python
import functools
import math

import jax
import jax.numpy as jnp
from jax import lax
from jax.experimental import pallas as pl
from jax.experimental.pallas import tpu as pltpu
from jax.sharding import PartitionSpec as P

beta_one = 0.9
beta_two = 0.999
learn_rate = 0.01
epsilon = 1e-08
bias_steps = 10.0

AXES = ("dp", "group")
Z, YH, CORE, X, YL = 8, 2, 2, 4, 4
GROUP = X * YL
PARTS = 4
root = math.sqrt(2.0 / math.pi)
cubic = 0.044715


def index(z, yh, c, x, yl):
    return ((z * YH + yh) * CORE + c) * GROUP + x * YL + yl


def places():
    for z in range(Z):
        for yh in range(YH):
            for c in range(CORE):
                for x in range(X):
                    for yl in range(YL):
                        yield z, yh, c, x, yl


def groups(key, order):
    held = {}
    for place in places():
        held.setdefault(key(*place), []).append((order(*place), index(*place)))
    return [[at for _, at in sorted(held[name])] for name in sorted(held)]


def run(at, c):
    return (at + 8 - 2 * c) % 8 // 4


OVER_GROUP = groups(lambda z, yh, c, x, yl: (z, c, run(yh * YL + yl, c)), lambda z, yh, c, x, yl: (x, yl))
OVER_XZ = groups(lambda z, yh, c, x, yl: (yh, yl, c, run(z, c)), lambda z, yh, c, x, yl: (x, z % PARTS))
OVER_Y = groups(lambda z, yh, c, x, yl: (z, c, x), lambda z, yh, c, x, yl: (yh, yl))
OVER_ZC = groups(lambda z, yh, c, x, yl: (yh, x, yl), lambda z, yh, c, x, yl: (c, z % PARTS, z // PARTS))
SWAP = [(index(z, yh, c, x, yl), index(z, yh, 1 - c, x, yl)) for z, yh, c, x, yl in places()]


def swap_cores(value):
    return lax.ppermute(value, AXES, SWAP)


def exchange(value, members):
    return lax.all_to_all(value, AXES, 0, 0, tiled=True, axis_index_groups=members)


def join_halves(core, own_ref, other_ref, out_ref, rows):
    own_at = core * rows
    other_at = rows - own_at
    for block in range(own_ref.shape[0] // rows):
        span = pl.ds(block * rows, rows)
        base = 2 * rows * block
        out_ref[pl.ds(pl.multiple_of(base + own_at, rows), rows), :] = own_ref[span, :]
        out_ref[pl.ds(pl.multiple_of(base + other_at, rows), rows), :] = other_ref[span, :]


def core_index():
    return lax.rem(lax.axis_index("dp"), CORE)


def forward_kernel(
    _, own_ref, other_ref, rows_ref, labels_ref, head_ref, weight_ref, dpre_ref, keep_ref, send_ref, flip_ref
):
    core = core_index()
    positions, piles, channels = rows_ref.shape
    outputs = head_ref.shape[1]
    classes = head_ref.shape[0]
    count = positions * piles
    join_halves(core, own_ref, other_ref, weight_ref, own_ref.shape[0] // GROUP)
    rows = rows_ref[...].reshape(count, channels)
    pre = jnp.dot(rows, weight_ref[...], preferred_element_type=jnp.float32)
    square = pre * pre
    bend = jnp.tanh(root * (pre + cubic * (pre * square)))
    act = 0.5 * pre * (1.0 + bend)
    slope = 0.5 * (1.0 + bend) + 0.5 * pre * (1.0 - bend * bend) * (root * (1.0 + 3.0 * cubic * square))
    pooled = act[:piles]
    for position in range(1, positions):
        pooled = pooled + act[position * piles : (position + 1) * piles]
    pooled = pooled / positions
    heads = [head_ref[kind : kind + 1, :] for kind in range(classes)]
    logits = [jnp.sum(pooled * vector, axis=1, keepdims=True) for vector in heads]
    top = functools.reduce(jnp.maximum, logits)
    powers = [jnp.exp(value - top) for value in logits]
    total = functools.reduce(jnp.add, powers)
    across = lax.broadcasted_iota(jnp.int32, (piles, piles), 0) == lax.broadcasted_iota(
        jnp.int32, (piles, piles), 1
    )
    marks = jnp.sum(
        jnp.where(across, labels_ref[...].astype(jnp.float32), 0.0), axis=1, keepdims=True
    )
    dpooled = jnp.zeros((piles, outputs), jnp.float32)
    for kind in range(classes):
        dlogit = powers[kind] / total - jnp.where(marks == float(kind), 1.0, 0.0)
        dpooled = dpooled + dlogit * heads[kind]
    dact = dpooled / positions
    dpre = jnp.concatenate([dact] * positions, axis=0) * slope
    dpre_ref[...] = dpre.astype(jnp.bfloat16)
    flip_ref[...] = dpre.T.astype(jnp.bfloat16)
    half = outputs // 2
    keep_ref[...] = flip_ref[pl.ds(pl.multiple_of(core * half, half), half), :]
    other = flip_ref[pl.ds(pl.multiple_of((1 - core) * half, half), half), :]
    gradient(other, rows_ref, send_ref)


def gradient(left, rows_ref, out_ref):
    positions, piles, channels = rows_ref.shape
    wide = channels // X
    width = wide // YL
    deep = left.shape[0] // PARTS
    for x in range(X):
        rows = rows_ref[:, :, x * wide : (x + 1) * wide].reshape(positions * piles, wide)
        product = jnp.dot(left, rows, preferred_element_type=jnp.float32).astype(out_ref.dtype)
        for part in range(PARTS):
            for yl in range(YL):
                out_ref[x, part, yl] = product[part * deep : (part + 1) * deep, yl * width : (yl + 1) * width]


def backward_kernel(weight_ref, rows_ref, dpre_ref, keep_ref, input_ref, grad_ref, held_ref, sems):
    positions, piles, channels = rows_ref.shape
    wide = channels // X
    copies = []
    for x in range(X):
        span = pl.ds(x * wide, wide)
        back = lax.dot_general(
            dpre_ref[...], weight_ref[span, :], (((1,), (1,)), ((), ())), preferred_element_type=jnp.float32
        )
        held_ref[:, :, span] = back.astype(jnp.bfloat16).reshape(positions, piles, wide)
        copies.append(
            pltpu.make_async_copy(held_ref.at[:, :, span], input_ref.at[:, :, span], sems.at[x])
        )
        copies[-1].start()
    gradient(keep_ref[...], rows_ref, grad_ref)
    for copy in copies:
        copy.wait()


def stage_kernel(_, weight_ref, first_ref, second_ref, out_weight, out_first, out_second):
    out_weight[...] = weight_ref[...]
    out_first[...] = first_ref[...]
    out_second[...] = second_ref[...]


def adam_kernel(parts_ref, weight_ref, first_ref, second_ref, out_weight, out_first, out_second):
    parts = [parts_ref[at].astype(jnp.float32) for at in range(parts_ref.shape[0])]
    sums = [parts[at] + parts[at + 1] for at in range(0, len(parts), 2)]
    grad = jnp.concatenate(sums, axis=0).T
    new_first = beta_one * first_ref[...] + (1.0 - beta_one) * grad
    new_second = beta_two * second_ref[...] + (1.0 - beta_two) * grad * grad
    first_hat = new_first / (1.0 - beta_one**bias_steps)
    second_hat = new_second / (1.0 - beta_two**bias_steps)
    out_weight[...] = weight_ref[...] - learn_rate * first_hat / (jnp.sqrt(second_hat) + epsilon)
    out_first[...] = new_first
    out_second[...] = new_second


def per_device(features, labels, weight, head, moment_one, moment_two):
    piles, positions, channels = features.shape
    shard, outputs = weight.shape
    count = piles * positions
    half_rows = shard // 2
    half_outs = outputs // 2
    core = lax.rem(lax.axis_index("dp"), CORE)
    rows = features.transpose(1, 0, 2)

    half = lax.dynamic_slice_in_dim(weight, core * half_rows, half_rows, 0).astype(jnp.bfloat16)
    copies = jnp.broadcast_to(half[None], (GROUP, half_rows, outputs)).reshape(-1, outputs)
    own = exchange(copies, OVER_GROUP)
    other = swap_cores(own)

    vmem = pl.BlockSpec(memory_space=pltpu.VMEM)
    anywhere = pl.BlockSpec(memory_space=pl.ANY)
    params = pltpu.CompilerParams(vmem_limit_bytes=16 << 20)
    staged = pl.pallas_call(
        stage_kernel,
        out_shape=(jax.ShapeDtypeStruct((shard, outputs), jnp.float32),) * 3,
        in_specs=[anywhere] + [vmem] * 3,
        out_specs=(vmem,) * 3,
        compiler_params=params,
        cost_estimate=pl.CostEstimate(flops=0, bytes_accessed=2 << 20, transcendentals=0),
        name="stage",
    )(own, weight, moment_one, moment_two)

    deep = half_outs // PARTS
    chunks = (X, PARTS, YL, deep, shard)
    joined, dpre, keep, send = pl.pallas_call(
        forward_kernel,
        out_shape=(
            jax.ShapeDtypeStruct((channels, outputs), jnp.bfloat16),
            jax.ShapeDtypeStruct((count, outputs), jnp.bfloat16),
            jax.ShapeDtypeStruct((half_outs, count), jnp.bfloat16),
            jax.ShapeDtypeStruct(chunks, jnp.bfloat16),
        ),
        in_specs=[anywhere] + [vmem] * 5,
        out_specs=(vmem,) * 4,
        scratch_shapes=[pltpu.VMEM((outputs, count), jnp.bfloat16)],
        compiler_params=params,
        cost_estimate=pl.CostEstimate(
            flops=3 * count * channels * outputs, bytes_accessed=4 << 20, transcendentals=count * outputs
        ),
        name="forward",
    )(staged[0], own, other, rows, labels.reshape(1, piles), head.T)

    received = swap_cores(send)
    input_grad, grad = pl.pallas_call(
        backward_kernel,
        out_shape=(
            jax.ShapeDtypeStruct((positions, piles, channels), jnp.bfloat16),
            jax.ShapeDtypeStruct(chunks, jnp.float32),
        ),
        in_specs=[vmem] * 4,
        out_specs=(anywhere, vmem),
        scratch_shapes=[
            pltpu.VMEM((positions, piles, channels), jnp.bfloat16),
            pltpu.SemaphoreType.DMA((X,)),
        ],
        compiler_params=params,
        cost_estimate=pl.CostEstimate(
            flops=3 * count * channels * outputs, bytes_accessed=6 << 20, transcendentals=0
        ),
        name="backward",
    )(joined, rows, dpre, keep)

    def total(parts, members):
        parts = parts.reshape(members, -1, deep, shard).astype(jnp.float32)
        return jnp.sum(parts, axis=0).astype(jnp.bfloat16)

    both = (grad + received.astype(jnp.float32)).astype(jnp.bfloat16).reshape(-1, YL, deep, shard)
    over_xz = total(exchange(both, OVER_XZ), X * PARTS)
    over_y = total(exchange(jnp.concatenate([over_xz] * YH, axis=0), OVER_Y), YH * YL)
    parts = exchange(jnp.broadcast_to(over_y, (Z * CORE, deep, shard)), OVER_ZC)

    new_weight, new_first, new_second = pl.pallas_call(
        adam_kernel,
        out_shape=(jax.ShapeDtypeStruct((shard, outputs), jnp.float32),) * 3,
        in_specs=[vmem] * 4,
        out_specs=(vmem,) * 3,
        compiler_params=params,
        name="adam",
    )(parts, *staged)
    return (input_grad.transpose(1, 0, 2), new_weight, new_first, new_second)


def solution(mesh):
    return jax.shard_map(
        per_device,
        mesh=mesh,
        in_specs=(
            P(("dp", "group"), None, None),
            P(("dp", "group")),
            P("group", None),
            P(),
            P("group", None),
            P("group", None),
        ),
        out_specs=(
            P(("dp", "group"), None, None),
            P("group", None),
            P("group", None),
            P("group", None),
        ),
        check_vma=False,
    )
```

```python
import functools
import math

import jax
import jax.numpy as jnp
from jax import lax
from jax.experimental import pallas as pl
from jax.experimental.pallas import tpu as pltpu
from jax.sharding import PartitionSpec as P

beta_one = 0.9
beta_two = 0.999
learn_rate = 0.01
epsilon = 1e-08
bias_steps = 10.0

AXES = ("dp", "group")
Z, YH, CORE, X, YL = 8, 2, 2, 4, 4
GROUP = X * YL
PAIR = 2
root = math.sqrt(2.0 / math.pi)
cubic = 0.044715


def index(z, yh, c, x, yl):
    return ((z * YH + yh) * CORE + c) * GROUP + x * YL + yl


def places():
    for z in range(Z):
        for yh in range(YH):
            for c in range(CORE):
                for x in range(X):
                    for yl in range(YL):
                        yield z, yh, c, x, yl


def groups(key, order):
    held = {}
    for place in places():
        held.setdefault(key(*place), []).append((order(*place), index(*place)))
    return [[at for _, at in sorted(held[name])] for name in sorted(held)]


OVER_XY = groups(lambda z, yh, c, x, yl: (z, yh, c, yl // PAIR), lambda z, yh, c, x, yl: (x, yl))
OVER_XYZ = groups(
    lambda z, yh, c, x, yl: (z // PAIR, yh, c, yl // PAIR), lambda z, yh, c, x, yl: (x, yl % PAIR, z % PAIR)
)
OVER_Y = groups(lambda z, yh, c, x, yl: (z, c, x, yl % PAIR), lambda z, yh, c, x, yl: (yh, yl))
OVER_Z = groups(lambda z, yh, c, x, yl: (yh, c, x, yl), lambda z, yh, c, x, yl: (z % PAIR, z))
SWAP = [(index(z, yh, c, x, yl), index(z, yh, 1 - c, x, yl)) for z, yh, c, x, yl in places()]
CROSS = [(index(z, yh, c, x, yl), index(z, yh, c, x, (yl + PAIR) % YL)) for z, yh, c, x, yl in places()]


def swap_cores(value):
    return lax.ppermute(value, AXES, SWAP)


def exchange(value, members):
    return lax.all_to_all(value, AXES, 0, 0, tiled=True, axis_index_groups=members)


def join_halves(core, own_ref, other_ref, out_ref, rows, places_of):
    own_at = core * rows
    other_at = rows - own_at
    for block, place in enumerate(places_of):
        span = pl.ds(block * rows, rows)
        base = 2 * rows * place
        out_ref[pl.ds(pl.multiple_of(base + own_at, rows), rows), :] = own_ref[span, :]
        out_ref[pl.ds(pl.multiple_of(base + other_at, rows), rows), :] = other_ref[span, :]


def core_index():
    return lax.rem(lax.axis_index("dp"), CORE)


def forward_kernel(
    _, own_ref, other_ref, rows_ref, labels_ref, head_ref, weight_ref, dpre_ref, keep_ref, send_ref, flip_ref
):
    core = core_index()
    positions, piles, channels = rows_ref.shape
    outputs = head_ref.shape[1]
    classes = head_ref.shape[0]
    count = positions * piles
    near = lax.rem(lax.axis_index("group"), YL) // PAIR
    shards = [
        x * YL + (near if turn == 0 else 1 - near) * PAIR + odd
        for x in range(X)
        for odd in range(PAIR)
        for turn in range(YL // PAIR)
    ]
    join_halves(core, own_ref, other_ref, weight_ref, own_ref.shape[0] // GROUP, shards)
    rows = rows_ref[...].reshape(count, channels)
    pre = jnp.dot(rows, weight_ref[...], preferred_element_type=jnp.float32)
    square = pre * pre
    bend = jnp.tanh(root * (pre + cubic * (pre * square)))
    act = 0.5 * pre * (1.0 + bend)
    slope = 0.5 * (1.0 + bend) + 0.5 * pre * (1.0 - bend * bend) * (root * (1.0 + 3.0 * cubic * square))
    pooled = act[:piles]
    for position in range(1, positions):
        pooled = pooled + act[position * piles : (position + 1) * piles]
    pooled = pooled / positions
    heads = [head_ref[kind : kind + 1, :] for kind in range(classes)]
    logits = [jnp.sum(pooled * vector, axis=1, keepdims=True) for vector in heads]
    top = functools.reduce(jnp.maximum, logits)
    powers = [jnp.exp(value - top) for value in logits]
    total = functools.reduce(jnp.add, powers)
    across = lax.broadcasted_iota(jnp.int32, (piles, piles), 0) == lax.broadcasted_iota(
        jnp.int32, (piles, piles), 1
    )
    marks = jnp.sum(
        jnp.where(across, labels_ref[...].astype(jnp.float32), 0.0), axis=1, keepdims=True
    )
    dpooled = jnp.zeros((piles, outputs), jnp.float32)
    for kind in range(classes):
        dlogit = powers[kind] / total - jnp.where(marks == float(kind), 1.0, 0.0)
        dpooled = dpooled + dlogit * heads[kind]
    dact = dpooled / positions
    dpre = jnp.concatenate([dact] * positions, axis=0) * slope
    dpre_ref[...] = dpre.astype(jnp.bfloat16)
    flip_ref[...] = dpre.T.astype(jnp.bfloat16)
    half = outputs // 2
    keep_ref[...] = flip_ref[pl.ds(pl.multiple_of(core * half, half), half), :]
    other = flip_ref[pl.ds(pl.multiple_of((1 - core) * half, half), half), :]
    gradient(other, rows_ref, send_ref)


def gradient(left, rows_ref, out_ref):
    positions, piles, channels = rows_ref.shape
    wide = channels // X
    width = wide // YL
    deep = left.shape[0] // PAIR
    for x in range(X):
        rows = rows_ref[:, :, x * wide : (x + 1) * wide].reshape(positions * piles, wide)
        product = jnp.dot(left, rows, preferred_element_type=jnp.float32).astype(out_ref.dtype)
        for part in range(PAIR):
            for yl in range(YL):
                out_ref[x, yl % PAIR, part, yl // PAIR] = product[
                    part * deep : (part + 1) * deep, yl * width : (yl + 1) * width
                ]


def backward_kernel(weight_ref, rows_ref, dpre_ref, keep_ref, input_ref, grad_ref, held_ref, sems):
    positions, piles, channels = rows_ref.shape
    wide = channels // X
    copies = []
    for x in range(X):
        span = pl.ds(x * wide, wide)
        back = lax.dot_general(
            dpre_ref[...], weight_ref[span, :], (((1,), (1,)), ((), ())), preferred_element_type=jnp.float32
        )
        held_ref[:, :, span] = back.astype(jnp.bfloat16).reshape(positions, piles, wide)
        copies.append(
            pltpu.make_async_copy(held_ref.at[:, :, span], input_ref.at[:, :, span], sems.at[x])
        )
        copies[-1].start()
    gradient(keep_ref[...], rows_ref, grad_ref)
    for copy in copies:
        copy.wait()


def stage_kernel(_, weight_ref, first_ref, second_ref, out_weight, out_first, out_second):
    out_weight[...] = weight_ref[...]
    out_first[...] = first_ref[...]
    out_second[...] = second_ref[...]


def adam_kernel(
    own_ref, other_ref, weight_ref, first_ref, second_ref, out_weight, out_first, out_second, flip_ref
):
    join_halves(core_index(), own_ref, other_ref, flip_ref, own_ref.shape[0], [0])
    grad = flip_ref[...].T
    new_first = beta_one * first_ref[...] + (1.0 - beta_one) * grad
    new_second = beta_two * second_ref[...] + (1.0 - beta_two) * grad * grad
    first_hat = new_first / (1.0 - beta_one**bias_steps)
    second_hat = new_second / (1.0 - beta_two**bias_steps)
    out_weight[...] = weight_ref[...] - learn_rate * first_hat / (jnp.sqrt(second_hat) + epsilon)
    out_first[...] = new_first
    out_second[...] = new_second


def per_device(features, labels, weight, head, moment_one, moment_two):
    piles, positions, channels = features.shape
    shard, outputs = weight.shape
    count = piles * positions
    half_rows = shard // 2
    half_outs = outputs // 2
    core = lax.rem(lax.axis_index("dp"), CORE)
    rows = features.transpose(1, 0, 2)

    half = lax.dynamic_slice_in_dim(weight, core * half_rows, half_rows, 0).astype(jnp.bfloat16)
    pair = jnp.concatenate([half, lax.ppermute(half, AXES, CROSS)], axis=0)
    copies = jnp.broadcast_to(pair[None], (X * PAIR, PAIR * half_rows, outputs))
    own = exchange(copies, OVER_XY).reshape(-1, outputs)
    other = swap_cores(own)

    vmem = pl.BlockSpec(memory_space=pltpu.VMEM)
    anywhere = pl.BlockSpec(memory_space=pl.ANY)
    params = pltpu.CompilerParams(vmem_limit_bytes=16 << 20)
    staged = pl.pallas_call(
        stage_kernel,
        out_shape=(jax.ShapeDtypeStruct((shard, outputs), jnp.float32),) * 3,
        in_specs=[anywhere] + [vmem] * 3,
        out_specs=(vmem,) * 3,
        compiler_params=params,
        cost_estimate=pl.CostEstimate(flops=0, bytes_accessed=2 << 20, transcendentals=0),
        name="stage",
    )(own, weight, moment_one, moment_two)

    deep = half_outs // PAIR
    chunks = (X, PAIR, PAIR, YL // PAIR, deep, shard)
    joined, dpre, keep, send = pl.pallas_call(
        forward_kernel,
        out_shape=(
            jax.ShapeDtypeStruct((channels, outputs), jnp.bfloat16),
            jax.ShapeDtypeStruct((count, outputs), jnp.bfloat16),
            jax.ShapeDtypeStruct((half_outs, count), jnp.bfloat16),
            jax.ShapeDtypeStruct(chunks, jnp.bfloat16),
        ),
        in_specs=[anywhere] + [vmem] * 5,
        out_specs=(vmem,) * 4,
        scratch_shapes=[pltpu.VMEM((outputs, count), jnp.bfloat16)],
        compiler_params=params,
        cost_estimate=pl.CostEstimate(
            flops=3 * count * channels * outputs, bytes_accessed=4 << 20, transcendentals=count * outputs
        ),
        name="forward",
    )(staged[0], own, other, rows, labels.reshape(1, piles), head.T)

    received = swap_cores(send)
    input_grad, grad = pl.pallas_call(
        backward_kernel,
        out_shape=(
            jax.ShapeDtypeStruct((positions, piles, channels), jnp.bfloat16),
            jax.ShapeDtypeStruct(chunks, jnp.float32),
        ),
        in_specs=[vmem] * 4,
        out_specs=(anywhere, vmem),
        scratch_shapes=[
            pltpu.VMEM((positions, piles, channels), jnp.bfloat16),
            pltpu.SemaphoreType.DMA((X,)),
        ],
        compiler_params=params,
        cost_estimate=pl.CostEstimate(
            flops=3 * count * channels * outputs, bytes_accessed=6 << 20, transcendentals=0
        ),
        name="backward",
    )(joined, rows, dpre, keep)

    both = (grad + received.astype(jnp.float32)).astype(jnp.bfloat16).reshape(GROUP, -1, deep, shard)
    over_xyz = jnp.sum(exchange(both, OVER_XYZ).astype(jnp.float32), axis=0).astype(jnp.bfloat16)
    copies = jnp.concatenate([over_xyz] * YH, axis=0)
    over_y = jnp.sum(exchange(copies, OVER_Y).astype(jnp.float32), axis=0).astype(jnp.bfloat16)
    parts = exchange(jnp.broadcast_to(over_y, (Z, deep, shard)), OVER_Z)
    mine = jnp.sum(parts.reshape(PAIR, Z // PAIR, deep, shard).astype(jnp.float32), axis=1)
    mine = mine.reshape(half_outs, shard)

    new_weight, new_first, new_second = pl.pallas_call(
        adam_kernel,
        out_shape=(jax.ShapeDtypeStruct((shard, outputs), jnp.float32),) * 3,
        in_specs=[vmem] * 5,
        out_specs=(vmem,) * 3,
        scratch_shapes=[pltpu.VMEM((outputs, shard), jnp.float32)],
        compiler_params=params,
        name="adam",
    )(mine, swap_cores(mine), *staged)
    return (input_grad.transpose(1, 0, 2), new_weight, new_first, new_second)


def solution(mesh):
    return jax.shard_map(
        per_device,
        mesh=mesh,
        in_specs=(
            P(("dp", "group"), None, None),
            P(("dp", "group")),
            P("group", None),
            P(),
            P("group", None),
            P("group", None),
        ),
        out_specs=(
            P(("dp", "group"), None, None),
            P("group", None),
            P("group", None),
            P("group", None),
        ),
        check_vma=False,
    )
```

```python
import functools
import math

import jax
import jax.numpy as jnp
from jax import lax
from jax.experimental import pallas as pl
from jax.experimental.pallas import tpu as pltpu
from jax.sharding import PartitionSpec as P

beta_one = 0.9
beta_two = 0.999
learn_rate = 0.01
epsilon = 1e-08
bias_steps = 10.0

AXES = ("dp", "group")
Z, YH, CORE, X, YL = 8, 2, 2, 4, 4
GROUP = X * YL
PAIR = 2
root = math.sqrt(2.0 / math.pi)
cubic = 0.044715


def index(z, yh, c, x, yl):
    return ((z * YH + yh) * CORE + c) * GROUP + x * YL + yl


def places():
    for z in range(Z):
        for yh in range(YH):
            for c in range(CORE):
                for x in range(X):
                    for yl in range(YL):
                        yield z, yh, c, x, yl


def groups(key, order):
    held = {}
    for place in places():
        held.setdefault(key(*place), []).append((order(*place), index(*place)))
    return [[at for _, at in sorted(held[name])] for name in sorted(held)]


OVER_XY = groups(lambda z, yh, c, x, yl: (z, yh, c, yl // PAIR), lambda z, yh, c, x, yl: (x, yl))
OVER_XYZ = groups(
    lambda z, yh, c, x, yl: (z // PAIR, yh, c, yl // PAIR), lambda z, yh, c, x, yl: (x, yl % PAIR, z % PAIR)
)
OVER_Y = groups(lambda z, yh, c, x, yl: (z, c, x, yl % PAIR), lambda z, yh, c, x, yl: (yh, yl))
OVER_Z = groups(lambda z, yh, c, x, yl: (yh, c, x, yl), lambda z, yh, c, x, yl: (z % PAIR, z))
SWAP = [(index(z, yh, c, x, yl), index(z, yh, 1 - c, x, yl)) for z, yh, c, x, yl in places()]


def beside(yh, yl):
    at = (yh * YL + yl + (1 if yl % PAIR else -1)) % (YH * YL)
    return at // YL, at % YL


CROSS = [(index(z, yh, c, x, yl), index(z, *beside(yh, yl)[:1], c, x, beside(yh, yl)[1])) for z, yh, c, x, yl in places()]


def swap_cores(value):
    return lax.ppermute(value, AXES, SWAP)


def exchange(value, members):
    return lax.all_to_all(value, AXES, 0, 0, tiled=True, axis_index_groups=members)


def core_index():
    return lax.rem(lax.axis_index("dp"), CORE)


def gelu_parts(pre):
    square = pre * pre
    bend = jnp.tanh(root * (pre + cubic * (pre * square)))
    act = 0.5 * pre * (1.0 + bend)
    slope = 0.5 * (1.0 + bend) + 0.5 * pre * (1.0 - bend * bend) * (root * (1.0 + 3.0 * cubic * square))
    return act, slope


def product(rows_ref, weight_ref):
    positions, piles, channels = rows_ref.shape
    return lax.dot_general(
        rows_ref[...].reshape(positions * piles, channels),
        weight_ref[...],
        (((1,), (1,)), ((), ())),
        preferred_element_type=jnp.float32,
    )


def head_half(head_ref, half):
    count = head_ref.shape[1] // 2
    whole = head_ref[...]
    chosen = jnp.where(half == 0, whole[:, :count], whole[:, count:])
    return [chosen[kind : kind + 1, :] for kind in range(head_ref.shape[0])]


def in_lanes(columns):
    lane = lax.broadcasted_iota(jnp.int32, (columns[0].shape[0], 128), 1)
    held = jnp.zeros(lane.shape, jnp.float32)
    for at, column in enumerate(columns):
        held = jnp.where(lane == at, column, held)
    return held


def spread(dlogits, heads, positions):
    dpooled = functools.reduce(jnp.add, [column * vector for column, vector in zip(dlogits, heads)])
    return jnp.concatenate([dpooled / positions] * positions, axis=0)


def prepare_kernel(weight_ref, out_ref, flip_ref):
    half = out_ref.shape[0]
    flip_ref[...] = weight_ref[...].T
    out_ref[...] = flip_ref[pl.ds(pl.multiple_of(core_index() * half, half), half), :].astype(jnp.bfloat16)


def forward_kernel(
    _, blocks_ref, rows_ref, others_ref, labels_ref, head_ref, weight_ref, slope_ref, logits_ref
):
    positions, piles, channels = rows_ref.shape
    width = channels // GROUP
    near = lax.rem(lax.axis_index("group"), YL) // PAIR
    for block in range(GROUP):
        yl = near * PAIR + block // 2 % PAIR
        shard = block // YL * YL + (yl if block % 2 == 0 else YL - 1 - yl)
        weight_ref[:, pl.ds(pl.multiple_of(shard * width, width), width)] = blocks_ref[block]
    heads = head_half(head_ref, core_index())
    across = lax.broadcasted_iota(jnp.int32, (piles, piles), 0) == lax.broadcasted_iota(
        jnp.int32, (piles, piles), 1
    )
    marks = jnp.sum(
        jnp.where(across, labels_ref[...].astype(jnp.float32), 0.0), axis=1, keepdims=True
    )
    for side, side_ref in enumerate((rows_ref, others_ref)):
        act, slope = gelu_parts(product(side_ref, weight_ref))
        slope_ref[side] = slope
        pooled = functools.reduce(
            jnp.add, [act[position * piles : (position + 1) * piles] for position in range(positions)]
        )
        pooled = pooled / positions
        logits = [jnp.sum(pooled * vector, axis=1, keepdims=True) for vector in heads]
        logits_ref[side] = in_lanes(logits + [marks] if side == 0 else logits)


def gradient_kernel(
    logits_ref, received_ref, slope_ref, rows_ref, others_ref, head_ref, grad_ref, dpre_ref, dlogits_ref
):
    positions, piles, channels = rows_ref.shape
    count = positions * piles
    classes = head_ref.shape[0]
    heads = head_half(head_ref, core_index())
    lefts = []
    for side in range(CORE):
        mine, theirs = logits_ref[side], received_ref[1 - side]
        marks = (mine if side == 0 else theirs)[:, classes : classes + 1]
        logits = [mine[:, kind : kind + 1] + theirs[:, kind : kind + 1] for kind in range(classes)]
        top = functools.reduce(jnp.maximum, logits)
        powers = [jnp.exp(value - top) for value in logits]
        total = functools.reduce(jnp.add, powers)
        dlogits = [
            powers[kind] / total - jnp.where(marks == float(kind), 1.0, 0.0) for kind in range(classes)
        ]
        dpre = spread(dlogits, heads, positions) * slope_ref[side]
        if side == 0:
            dpre_ref[...] = dpre.astype(jnp.bfloat16)
            dlogits_ref[...] = in_lanes(dlogits)
        lefts.append(dpre.T.astype(jnp.bfloat16))
    wide = channels // X
    width = wide // YL
    deep = lefts[0].shape[0] // PAIR
    for x in range(X):
        parts = [
            jnp.dot(
                left,
                side_ref[:, :, x * wide : (x + 1) * wide].reshape(count, wide),
                preferred_element_type=jnp.float32,
            )
            for left, side_ref in zip(lefts, (rows_ref, others_ref))
        ]
        total = (parts[0] + parts[1]).astype(jnp.bfloat16)
        for part in range(PAIR):
            for yl in range(YL):
                grad_ref[x, yl % PAIR, part, yl // PAIR] = total[
                    part * deep : (part + 1) * deep, yl * width : (yl + 1) * width
                ]


def input_kernel(
    _, weight_ref, other_ref, rows_ref, dpre_ref, dlogits_ref, head_ref, input_ref, held_ref, sems
):
    positions, piles, channels = rows_ref.shape
    heads = head_half(head_ref, 1 - core_index())
    slope = gelu_parts(product(rows_ref, other_ref))[1]
    dlogits = [dlogits_ref[:, kind : kind + 1] for kind in range(head_ref.shape[0])]
    rest = (spread(dlogits, heads, positions) * slope).astype(jnp.bfloat16)
    wide = channels // X
    copies = []
    for x in range(X):
        span = pl.ds(x * wide, wide)
        back = jnp.dot(dpre_ref[...], weight_ref[:, span], preferred_element_type=jnp.float32)
        back = back + jnp.dot(rest, other_ref[:, span], preferred_element_type=jnp.float32)
        held_ref[:, :, span] = back.astype(jnp.bfloat16).reshape(positions, piles, wide)
        copies.append(
            pltpu.make_async_copy(held_ref.at[:, :, span], input_ref.at[:, :, span], sems.at[x])
        )
        copies[-1].start()
    for copy in copies:
        copy.wait()


def stage_kernel(_, weight_ref, first_ref, second_ref, out_weight, out_first, out_second):
    out_weight[...] = weight_ref[...]
    out_first[...] = first_ref[...]
    out_second[...] = second_ref[...]


def adam_kernel(
    _, own_ref, other_ref, weight_ref, first_ref, second_ref, out_weight, out_first, out_second, flip_ref
):
    half = own_ref.shape[0]
    core = core_index()
    flip_ref[pl.ds(pl.multiple_of(core * half, half), half), :] = own_ref[...]
    flip_ref[pl.ds(pl.multiple_of((1 - core) * half, half), half), :] = other_ref[...]
    grad = flip_ref[...].T
    new_first = beta_one * first_ref[...] + (1.0 - beta_one) * grad
    new_second = beta_two * second_ref[...] + (1.0 - beta_two) * grad * grad
    first_hat = new_first / (1.0 - beta_one**bias_steps)
    second_hat = new_second / (1.0 - beta_two**bias_steps)
    out_weight[...] = weight_ref[...] - learn_rate * first_hat / (jnp.sqrt(second_hat) + epsilon)
    out_first[...] = new_first
    out_second[...] = new_second


def per_device(features, labels, weight, head, moment_one, moment_two):
    piles, positions, channels = features.shape
    shard, outputs = weight.shape
    count = piles * positions
    half_outs = outputs // 2
    deep = half_outs // PAIR
    rows = features.transpose(1, 0, 2)
    flat_head = head.T
    vmem = pl.BlockSpec(memory_space=pltpu.VMEM)
    anywhere = pl.BlockSpec(memory_space=pl.ANY)
    params = pltpu.CompilerParams(vmem_limit_bytes=16 << 20)

    half = pl.pallas_call(
        prepare_kernel,
        out_shape=jax.ShapeDtypeStruct((half_outs, shard), jnp.bfloat16),
        in_specs=[vmem],
        out_specs=vmem,
        scratch_shapes=[pltpu.VMEM((outputs, shard), jnp.float32)],
        compiler_params=params,
        name="prepare",
    )(weight)
    pair = jnp.stack([half, lax.ppermute(half, AXES, CROSS)])
    sent_rows, half = lax.optimization_barrier((rows, half))
    other_rows = swap_cores(sent_rows)
    staged = pl.pallas_call(
        stage_kernel,
        out_shape=(jax.ShapeDtypeStruct((shard, outputs), jnp.float32),) * 3,
        in_specs=[anywhere] + [vmem] * 3,
        out_specs=(vmem,) * 3,
        compiler_params=params,
        cost_estimate=pl.CostEstimate(flops=0, bytes_accessed=2 << 20, transcendentals=0),
        name="stage",
    )(half, weight, moment_one, moment_two)
    copies = jnp.broadcast_to(pair, (X * PAIR, PAIR, half_outs, shard))
    blocks = exchange(copies, OVER_XY).reshape(GROUP, half_outs, shard)

    flops = 2 * count * channels * outputs
    weight_half, slope, logits = pl.pallas_call(
        forward_kernel,
        out_shape=(
            jax.ShapeDtypeStruct((half_outs, channels), jnp.bfloat16),
            jax.ShapeDtypeStruct((CORE, count, half_outs), jnp.float32),
            jax.ShapeDtypeStruct((CORE, piles, 128), jnp.float32),
        ),
        in_specs=[anywhere] + [vmem] * 5,
        out_specs=(vmem,) * 3,
        compiler_params=params,
        cost_estimate=pl.CostEstimate(
            flops=flops, bytes_accessed=4 << 20, transcendentals=count * outputs
        ),
        name="forward",
    )(staged[0], blocks, rows, other_rows, labels.reshape(1, piles), flat_head)

    received = swap_cores(logits)
    other_half = swap_cores(weight_half)
    grad, dpre, dlogits = pl.pallas_call(
        gradient_kernel,
        out_shape=(
            jax.ShapeDtypeStruct((X, PAIR, PAIR, YL // PAIR, deep, shard), jnp.bfloat16),
            jax.ShapeDtypeStruct((count, half_outs), jnp.bfloat16),
            jax.ShapeDtypeStruct((piles, 128), jnp.float32),
        ),
        in_specs=[vmem] * 6,
        out_specs=(vmem,) * 3,
        compiler_params=params,
        cost_estimate=pl.CostEstimate(flops=flops, bytes_accessed=4 << 20, transcendentals=0),
        name="gradient",
    )(logits, received, slope, rows, other_rows, flat_head)

    both = grad.reshape(GROUP, -1, deep, shard)
    over_xyz = jnp.sum(exchange(both, OVER_XYZ).astype(jnp.float32), axis=0).astype(jnp.bfloat16)
    copies = jnp.concatenate([over_xyz] * YH, axis=0)
    over_y = jnp.sum(exchange(copies, OVER_Y).astype(jnp.float32), axis=0).astype(jnp.bfloat16)
    parts = exchange(jnp.broadcast_to(over_y, (Z, deep, shard)), OVER_Z)
    mine = jnp.sum(parts.reshape(PAIR, Z // PAIR, deep, shard).astype(jnp.float32), axis=1)
    mine = mine.reshape(half_outs, shard)

    theirs = swap_cores(mine)
    input_grad = pl.pallas_call(
        input_kernel,
        out_shape=jax.ShapeDtypeStruct((positions, piles, channels), jnp.bfloat16),
        in_specs=[anywhere] + [vmem] * 6,
        out_specs=anywhere,
        scratch_shapes=[
            pltpu.VMEM((positions, piles, channels), jnp.bfloat16),
            pltpu.SemaphoreType.DMA((X,)),
        ],
        compiler_params=params,
        cost_estimate=pl.CostEstimate(
            flops=flops, bytes_accessed=4 << 20, transcendentals=count * outputs
        ),
        name="input_grad",
    )(mine, weight_half, other_half, rows, dpre, dlogits, flat_head)

    new_weight, new_first, new_second = pl.pallas_call(
        adam_kernel,
        out_shape=(jax.ShapeDtypeStruct((shard, outputs), jnp.float32),) * 3,
        in_specs=[anywhere] + [vmem] * 5,
        out_specs=(vmem,) * 3,
        scratch_shapes=[pltpu.VMEM((outputs, shard), jnp.float32)],
        compiler_params=params,
        name="adam",
    )(input_grad, mine, theirs, *staged)
    return (input_grad.transpose(1, 0, 2), new_weight, new_first, new_second)


def solution(mesh):
    return jax.shard_map(
        per_device,
        mesh=mesh,
        in_specs=(
            P(("dp", "group"), None, None),
            P(("dp", "group")),
            P("group", None),
            P(),
            P("group", None),
            P("group", None),
        ),
        out_specs=(
            P(("dp", "group"), None, None),
            P("group", None),
            P("group", None),
            P("group", None),
        ),
        check_vma=False,
    )
```

```python
import functools
import math

import jax
import jax.numpy as jnp
from jax import lax
from jax.experimental import pallas as pl
from jax.experimental.pallas import tpu as pltpu
from jax.sharding import PartitionSpec as P

beta_one = 0.9
beta_two = 0.999
learn_rate = 0.01
epsilon = 1e-08
bias_steps = 10.0

AXES = ("dp", "group")
Z, YH, CORE, X, YL = 8, 2, 2, 4, 4
GROUP = X * YL
PAIR = 2
root = math.sqrt(2.0 / math.pi)
cubic = 0.044715


def index(z, yh, c, x, yl):
    return ((z * YH + yh) * CORE + c) * GROUP + x * YL + yl


def places():
    for z in range(Z):
        for yh in range(YH):
            for c in range(CORE):
                for x in range(X):
                    for yl in range(YL):
                        yield z, yh, c, x, yl


def groups(key, order):
    held = {}
    for place in places():
        held.setdefault(key(*place), []).append((order(*place), index(*place)))
    return [[at for _, at in sorted(held[name])] for name in sorted(held)]


OVER_XY = groups(lambda z, yh, c, x, yl: (z, yh, c, yl // PAIR), lambda z, yh, c, x, yl: (x, yl))
OVER_XYZ = groups(
    lambda z, yh, c, x, yl: (z // PAIR, yh, c, yl // PAIR), lambda z, yh, c, x, yl: (x, yl % PAIR, z % PAIR)
)
OVER_Y = groups(lambda z, yh, c, x, yl: (z, c, x, yl % PAIR), lambda z, yh, c, x, yl: (yh, yl))
OVER_Z = groups(lambda z, yh, c, x, yl: (yh, c, x, yl), lambda z, yh, c, x, yl: (z % PAIR, z))
SWAP = [(index(z, yh, c, x, yl), index(z, yh, 1 - c, x, yl)) for z, yh, c, x, yl in places()]


def beside(yh, yl):
    at = (yh * YL + yl + (1 if yl % PAIR else -1)) % (YH * YL)
    return at // YL, at % YL


CROSS = [(index(z, yh, c, x, yl), index(z, *beside(yh, yl)[:1], c, x, beside(yh, yl)[1])) for z, yh, c, x, yl in places()]


def swap_cores(value):
    return lax.ppermute(value, AXES, SWAP)


def exchange(value, members):
    return lax.all_to_all(value, AXES, 0, 0, tiled=True, axis_index_groups=members)


def core_index():
    return lax.rem(lax.axis_index("dp"), CORE)


def gelu_parts(pre):
    square = pre * pre
    bend = jnp.tanh(root * (pre + cubic * (pre * square)))
    act = 0.5 * pre * (1.0 + bend)
    slope = 0.5 * (1.0 + bend) + 0.5 * pre * (1.0 - bend * bend) * (root * (1.0 + 3.0 * cubic * square))
    return act, slope


def product(rows_ref, weight_ref):
    positions, piles, channels = rows_ref.shape
    return lax.dot_general(
        rows_ref[...].reshape(positions * piles, channels),
        weight_ref[...],
        (((1,), (1,)), ((), ())),
        preferred_element_type=jnp.float32,
    )


def head_half(head_ref, half):
    count = head_ref.shape[1] // 2
    whole = head_ref[...]
    chosen = jnp.where(half == 0, whole[:, :count], whole[:, count:])
    return [chosen[kind : kind + 1, :] for kind in range(head_ref.shape[0])]


def in_lanes(columns):
    lane = lax.broadcasted_iota(jnp.int32, (columns[0].shape[0], 128), 1)
    held = jnp.zeros(lane.shape, jnp.float32)
    for at, column in enumerate(columns):
        held = jnp.where(lane == at, column, held)
    return held


def spread(dlogits, heads, positions):
    dpooled = functools.reduce(jnp.add, [column * vector for column, vector in zip(dlogits, heads)])
    return jnp.concatenate([dpooled / positions] * positions, axis=0)


def prepare_kernel(weight_ref, out_ref, flip_ref):
    half = out_ref.shape[0]
    flip_ref[...] = weight_ref[...].T
    out_ref[...] = flip_ref[pl.ds(pl.multiple_of(core_index() * half, half), half), :].astype(jnp.bfloat16)


def assemble(blocks_ref, weight_ref):
    width = blocks_ref.shape[2]
    near = lax.rem(lax.axis_index("group"), YL) // PAIR
    for block in range(GROUP):
        yl = near * PAIR + block // 2 % PAIR
        shard = block // YL * YL + (yl if block % 2 == 0 else YL - 1 - yl)
        weight_ref[:, pl.ds(pl.multiple_of(shard * width, width), width)] = blocks_ref[block]


def forward_kernel(
    blocks_ref, rows_ref, others_ref, labels_ref, head_ref, slope_ref, logits_ref, weight_ref
):
    positions, piles, channels = rows_ref.shape
    assemble(blocks_ref, weight_ref)
    heads = head_half(head_ref, core_index())
    across = lax.broadcasted_iota(jnp.int32, (piles, piles), 0) == lax.broadcasted_iota(
        jnp.int32, (piles, piles), 1
    )
    marks = jnp.sum(
        jnp.where(across, labels_ref[...].astype(jnp.float32), 0.0), axis=1, keepdims=True
    )
    for side, side_ref in enumerate((rows_ref, others_ref)):
        act, slope = gelu_parts(product(side_ref, weight_ref))
        slope_ref[side] = slope
        pooled = functools.reduce(
            jnp.add, [act[position * piles : (position + 1) * piles] for position in range(positions)]
        )
        pooled = pooled / positions
        logits = [jnp.sum(pooled * vector, axis=1, keepdims=True) for vector in heads]
        logits_ref[side] = in_lanes(logits + [marks] if side == 0 else logits)


def gradient_kernel(
    logits_ref, received_ref, slope_ref, rows_ref, others_ref, head_ref, grad_ref, dpre_ref, dlogits_ref
):
    positions, piles, channels = rows_ref.shape
    count = positions * piles
    classes = head_ref.shape[0]
    heads = head_half(head_ref, core_index())
    lefts = []
    for side in range(CORE):
        mine, theirs = logits_ref[side], received_ref[1 - side]
        marks = (mine if side == 0 else theirs)[:, classes : classes + 1]
        logits = [mine[:, kind : kind + 1] + theirs[:, kind : kind + 1] for kind in range(classes)]
        top = functools.reduce(jnp.maximum, logits)
        powers = [jnp.exp(value - top) for value in logits]
        total = functools.reduce(jnp.add, powers)
        dlogits = [
            powers[kind] / total - jnp.where(marks == float(kind), 1.0, 0.0) for kind in range(classes)
        ]
        dpre = spread(dlogits, heads, positions) * slope_ref[side]
        if side == 0:
            dpre_ref[...] = dpre.astype(jnp.bfloat16)
            dlogits_ref[...] = in_lanes(dlogits)
        lefts.append(dpre.T.astype(jnp.bfloat16))
    wide = channels // X
    width = wide // YL
    deep = lefts[0].shape[0] // PAIR
    for x in range(X):
        parts = [
            jnp.dot(
                left,
                side_ref[:, :, x * wide : (x + 1) * wide].reshape(count, wide),
                preferred_element_type=jnp.float32,
            )
            for left, side_ref in zip(lefts, (rows_ref, others_ref))
        ]
        total = (parts[0] + parts[1]).astype(jnp.bfloat16)
        for part in range(PAIR):
            for yl in range(YL):
                grad_ref[x, yl % PAIR, part, yl // PAIR] = total[
                    part * deep : (part + 1) * deep, yl * width : (yl + 1) * width
                ]


def sum_kernel(parts_ref, out_ref):
    count, rows = parts_ref.shape[:2]
    total = parts_ref[0].astype(jnp.float32)
    for at in range(1, count):
        total = total + parts_ref[at].astype(jnp.float32)
    for copy in range(out_ref.shape[0] // rows):
        out_ref[copy * rows : (copy + 1) * rows] = total.astype(jnp.bfloat16)


def input_kernel(
    blocks_ref, others_ref, rows_ref, dpre_ref, dlogits_ref, head_ref, input_ref, weight_ref, other_ref, held_ref, sems
):
    positions, piles, channels = rows_ref.shape
    assemble(blocks_ref, weight_ref)
    assemble(others_ref, other_ref)
    heads = head_half(head_ref, 1 - core_index())
    slope = gelu_parts(product(rows_ref, other_ref))[1]
    dlogits = [dlogits_ref[:, kind : kind + 1] for kind in range(head_ref.shape[0])]
    rest = (spread(dlogits, heads, positions) * slope).astype(jnp.bfloat16)
    wide = channels // X
    copies = []
    for x in range(X):
        span = pl.ds(x * wide, wide)
        back = jnp.dot(dpre_ref[...], weight_ref[:, span], preferred_element_type=jnp.float32)
        back = back + jnp.dot(rest, other_ref[:, span], preferred_element_type=jnp.float32)
        held_ref[:, :, span] = back.astype(jnp.bfloat16).reshape(positions, piles, wide)
        copies.append(
            pltpu.make_async_copy(held_ref.at[:, :, span], input_ref.at[:, :, span], sems.at[x])
        )
        copies[-1].start()
    for copy in copies:
        copy.wait()


def adam_kernel(
    own_ref, other_ref, weight_ref, first_ref, second_ref, out_weight, out_first, out_second, flip_ref
):
    half = own_ref.shape[0]
    core = core_index()
    flip_ref[pl.ds(pl.multiple_of(core * half, half), half), :] = own_ref[...]
    flip_ref[pl.ds(pl.multiple_of((1 - core) * half, half), half), :] = other_ref[...]
    grad = flip_ref[...].T
    new_first = beta_one * first_ref[...] + (1.0 - beta_one) * grad
    new_second = beta_two * second_ref[...] + (1.0 - beta_two) * grad * grad
    first_hat = new_first / (1.0 - beta_one**bias_steps)
    second_hat = new_second / (1.0 - beta_two**bias_steps)
    out_weight[...] = weight_ref[...] - learn_rate * first_hat / (jnp.sqrt(second_hat) + epsilon)
    out_first[...] = new_first
    out_second[...] = new_second


def per_device(features, labels, weight, head, moment_one, moment_two):
    piles, positions, channels = features.shape
    shard, outputs = weight.shape
    count = piles * positions
    half_outs = outputs // 2
    deep = half_outs // PAIR
    rows = features.transpose(1, 0, 2)
    flat_head = head.T
    vmem = pl.BlockSpec(memory_space=pltpu.VMEM)
    anywhere = pl.BlockSpec(memory_space=pl.ANY)
    params = pltpu.CompilerParams(vmem_limit_bytes=16 << 20)

    half = pl.pallas_call(
        prepare_kernel,
        out_shape=jax.ShapeDtypeStruct((half_outs, shard), jnp.bfloat16),
        in_specs=[vmem],
        out_specs=vmem,
        scratch_shapes=[pltpu.VMEM((outputs, shard), jnp.float32)],
        compiler_params=params,
        name="prepare",
    )(weight)
    pair = jnp.stack([half, lax.ppermute(half, AXES, CROSS)])
    sent_rows, pair = lax.optimization_barrier((rows, pair))
    other_rows = swap_cores(sent_rows)
    copies = jnp.broadcast_to(pair, (X * PAIR, PAIR, half_outs, shard))
    blocks = exchange(copies, OVER_XY).reshape(GROUP, half_outs, shard)

    flops = 2 * count * channels * outputs
    slope, logits = pl.pallas_call(
        forward_kernel,
        out_shape=(
            jax.ShapeDtypeStruct((CORE, count, half_outs), jnp.float32),
            jax.ShapeDtypeStruct((CORE, piles, 128), jnp.float32),
        ),
        in_specs=[vmem] * 5,
        out_specs=(vmem,) * 2,
        scratch_shapes=[pltpu.VMEM((half_outs, channels), jnp.bfloat16)],
        compiler_params=params,
        cost_estimate=pl.CostEstimate(
            flops=flops, bytes_accessed=4 << 20, transcendentals=count * outputs
        ),
        name="forward",
    )(blocks, rows, other_rows, labels.reshape(1, piles), flat_head)

    received = swap_cores(logits)
    grad, dpre, dlogits = pl.pallas_call(
        gradient_kernel,
        out_shape=(
            jax.ShapeDtypeStruct((X, PAIR, PAIR, YL // PAIR, deep, shard), jnp.bfloat16),
            jax.ShapeDtypeStruct((count, half_outs), jnp.bfloat16),
            jax.ShapeDtypeStruct((piles, 128), jnp.float32),
        ),
        in_specs=[vmem] * 6,
        out_specs=(vmem,) * 3,
        compiler_params=params,
        cost_estimate=pl.CostEstimate(flops=flops, bytes_accessed=4 << 20, transcendentals=0),
        name="gradient",
    )(logits, received, slope, rows, other_rows, flat_head)

    both = grad.reshape(GROUP, -1, deep, shard)
    parts = exchange(both, OVER_XYZ)
    other_blocks = swap_cores(blocks)
    input_grad = pl.pallas_call(
        input_kernel,
        out_shape=jax.ShapeDtypeStruct((positions, piles, channels), jnp.bfloat16),
        in_specs=[vmem] * 6,
        out_specs=anywhere,
        scratch_shapes=[
            pltpu.VMEM((half_outs, channels), jnp.bfloat16),
            pltpu.VMEM((half_outs, channels), jnp.bfloat16),
            pltpu.VMEM((positions, piles, channels), jnp.bfloat16),
            pltpu.SemaphoreType.DMA((X,)),
        ],
        compiler_params=params,
        cost_estimate=pl.CostEstimate(
            flops=flops, bytes_accessed=4 << 20, transcendentals=count * outputs
        ),
        name="input_grad",
    )(blocks, other_blocks, rows, dpre, dlogits, flat_head)
    parts, input_grad = lax.optimization_barrier((parts, input_grad))
    copies = pl.pallas_call(
        sum_kernel,
        out_shape=jax.ShapeDtypeStruct((YH * parts.shape[1], deep, shard), jnp.bfloat16),
        in_specs=[vmem],
        out_specs=vmem,
        compiler_params=params,
        name="sum",
    )(parts)
    over_y = jnp.sum(exchange(copies, OVER_Y).astype(jnp.float32), axis=0).astype(jnp.bfloat16)
    parts = exchange(jnp.broadcast_to(over_y, (Z, deep, shard)), OVER_Z)
    mine = jnp.sum(parts.reshape(PAIR, Z // PAIR, deep, shard).astype(jnp.float32), axis=1)
    mine = mine.reshape(half_outs, shard)

    theirs = swap_cores(mine)
    new_weight, new_first, new_second = pl.pallas_call(
        adam_kernel,
        out_shape=(jax.ShapeDtypeStruct((shard, outputs), jnp.float32),) * 3,
        in_specs=[vmem] * 5,
        out_specs=(vmem,) * 3,
        scratch_shapes=[pltpu.VMEM((outputs, shard), jnp.float32)],
        compiler_params=params,
        name="adam",
    )(mine, theirs, weight, moment_one, moment_two)
    return (input_grad.transpose(1, 0, 2), new_weight, new_first, new_second)


def solution(mesh):
    return jax.shard_map(
        per_device,
        mesh=mesh,
        in_specs=(
            P(("dp", "group"), None, None),
            P(("dp", "group")),
            P("group", None),
            P(),
            P("group", None),
            P("group", None),
        ),
        out_specs=(
            P(("dp", "group"), None, None),
            P("group", None),
            P("group", None),
            P("group", None),
        ),
        check_vma=False,
    )
```

```python
import functools
import math

import jax
import jax.numpy as jnp
from jax import lax
from jax.experimental import pallas as pl
from jax.experimental.pallas import tpu as pltpu
from jax.sharding import PartitionSpec as P

beta_one = 0.9
beta_two = 0.999
learn_rate = 0.01
epsilon = 1e-08
bias_steps = 10.0

AXES = ("dp", "group")
Z, YH, CORE, X, YL = 8, 2, 2, 4, 4
GROUP = X * YL
PAIR = 2
root = math.sqrt(2.0 / math.pi)
cubic = 0.044715


def index(z, yh, c, x, yl):
    return ((z * YH + yh) * CORE + c) * GROUP + x * YL + yl


def places():
    for z in range(Z):
        for yh in range(YH):
            for c in range(CORE):
                for x in range(X):
                    for yl in range(YL):
                        yield z, yh, c, x, yl


def groups(key, order):
    held = {}
    for place in places():
        held.setdefault(key(*place), []).append((order(*place), index(*place)))
    return [[at for _, at in sorted(held[name])] for name in sorted(held)]


OVER_XY = groups(lambda z, yh, c, x, yl: (z, yh, c, yl // PAIR), lambda z, yh, c, x, yl: (x, yl))
OVER_XYZ = groups(
    lambda z, yh, c, x, yl: (z // PAIR, yh, c, yl // PAIR), lambda z, yh, c, x, yl: (x, yl % PAIR, z % PAIR)
)
OVER_Y = groups(lambda z, yh, c, x, yl: (z, c, x, yl % PAIR), lambda z, yh, c, x, yl: (yh, yl))
OVER_Z = groups(lambda z, yh, c, x, yl: (yh, c, x, yl), lambda z, yh, c, x, yl: (z % PAIR, z))
SWAP = [(index(z, yh, c, x, yl), index(z, yh, 1 - c, x, yl)) for z, yh, c, x, yl in places()]


def beside(yh, yl):
    at = (yh * YL + yl + (1 if yl % PAIR else -1)) % (YH * YL)
    return at // YL, at % YL


CROSS = [(index(z, yh, c, x, yl), index(z, *beside(yh, yl)[:1], c, x, beside(yh, yl)[1])) for z, yh, c, x, yl in places()]


def swap_cores(value):
    return lax.ppermute(value, AXES, SWAP)


def exchange(value, members):
    return lax.all_to_all(value, AXES, 0, 0, tiled=True, axis_index_groups=members)


def core_index():
    return lax.rem(lax.axis_index("dp"), CORE)


def gelu_parts(pre):
    square = pre * pre
    bend = jnp.tanh(root * (pre + cubic * (pre * square)))
    act = 0.5 * pre * (1.0 + bend)
    slope = 0.5 * (1.0 + bend) + 0.5 * pre * (1.0 - bend * bend) * (root * (1.0 + 3.0 * cubic * square))
    return act, slope


def product(rows_ref, weight_ref):
    positions, piles, channels = rows_ref.shape
    return lax.dot_general(
        rows_ref[...].reshape(positions * piles, channels),
        weight_ref[...],
        (((1,), (1,)), ((), ())),
        preferred_element_type=jnp.float32,
    )


def head_half(head_ref, half):
    count = head_ref.shape[1] // 2
    whole = head_ref[...]
    chosen = jnp.where(half == 0, whole[:, :count], whole[:, count:])
    return [chosen[kind : kind + 1, :] for kind in range(head_ref.shape[0])]


def in_lanes(columns):
    lane = lax.broadcasted_iota(jnp.int32, (columns[0].shape[0], 128), 1)
    held = jnp.zeros(lane.shape, jnp.float32)
    for at, column in enumerate(columns):
        held = jnp.where(lane == at, column, held)
    return held


def spread(dlogits, heads, positions):
    dpooled = functools.reduce(jnp.add, [column * vector for column, vector in zip(dlogits, heads)])
    return jnp.concatenate([dpooled / positions] * positions, axis=0)


def prepare_kernel(weight_ref, out_ref, flip_ref):
    half = out_ref.shape[0]
    flip_ref[...] = weight_ref[...].T
    out_ref[...] = flip_ref[pl.ds(pl.multiple_of(core_index() * half, half), half), :].astype(jnp.bfloat16)


def assemble(blocks_ref, weight_ref):
    width = blocks_ref.shape[2]
    near = lax.rem(lax.axis_index("group"), YL) // PAIR
    for block in range(GROUP):
        yl = near * PAIR + block // 2 % PAIR
        shard = block // YL * YL + (yl if block % 2 == 0 else YL - 1 - yl)
        weight_ref[:, pl.ds(pl.multiple_of(shard * width, width), width)] = blocks_ref[block]


def forward_kernel(
    blocks_ref, rows_ref, others_ref, labels_ref, head_ref, slope_ref, logits_ref, weight_ref
):
    positions, piles, channels = rows_ref.shape
    assemble(blocks_ref, weight_ref)
    heads = head_half(head_ref, core_index())
    across = lax.broadcasted_iota(jnp.int32, (piles, piles), 0) == lax.broadcasted_iota(
        jnp.int32, (piles, piles), 1
    )
    marks = jnp.sum(
        jnp.where(across, labels_ref[...].astype(jnp.float32), 0.0), axis=1, keepdims=True
    )
    for side, side_ref in enumerate((rows_ref, others_ref)):
        act, slope = gelu_parts(product(side_ref, weight_ref))
        slope_ref[side] = slope
        pooled = functools.reduce(
            jnp.add, [act[position * piles : (position + 1) * piles] for position in range(positions)]
        )
        pooled = pooled / positions
        logits = [jnp.sum(pooled * vector, axis=1, keepdims=True) for vector in heads]
        logits_ref[side] = in_lanes(logits + [marks] if side == 0 else logits)


def gradient_kernel(
    logits_ref, received_ref, slope_ref, rows_ref, others_ref, head_ref, grad_ref, dlogits_ref
):
    positions, piles, channels = rows_ref.shape
    count = positions * piles
    classes = head_ref.shape[0]
    heads = head_half(head_ref, core_index())
    lefts = []
    for side in range(CORE):
        mine, theirs = logits_ref[side], received_ref[1 - side]
        marks = (mine if side == 0 else theirs)[:, classes : classes + 1]
        logits = [mine[:, kind : kind + 1] + theirs[:, kind : kind + 1] for kind in range(classes)]
        top = functools.reduce(jnp.maximum, logits)
        powers = [jnp.exp(value - top) for value in logits]
        total = functools.reduce(jnp.add, powers)
        dlogits = [
            powers[kind] / total - jnp.where(marks == float(kind), 1.0, 0.0) for kind in range(classes)
        ]
        dpre = spread(dlogits, heads, positions) * slope_ref[side]
        if side == 0:
            dlogits_ref[...] = in_lanes(dlogits)
        lefts.append(dpre.T.astype(jnp.bfloat16))
    wide = channels // X
    width = wide // YL
    deep = lefts[0].shape[0] // PAIR
    for x in range(X):
        parts = [
            jnp.dot(
                left,
                side_ref[:, :, x * wide : (x + 1) * wide].reshape(count, wide),
                preferred_element_type=jnp.float32,
            )
            for left, side_ref in zip(lefts, (rows_ref, others_ref))
        ]
        total = (parts[0] + parts[1]).astype(jnp.bfloat16)
        for part in range(PAIR):
            for yl in range(YL):
                grad_ref[x, yl % PAIR, part, yl // PAIR] = total[
                    part * deep : (part + 1) * deep, yl * width : (yl + 1) * width
                ]


def sum_kernel(parts_ref, out_ref):
    count, rows = parts_ref.shape[:2]
    total = parts_ref[0].astype(jnp.float32)
    for at in range(1, count):
        total = total + parts_ref[at].astype(jnp.float32)
    for copy in range(out_ref.shape[0] // rows):
        out_ref[copy * rows : (copy + 1) * rows] = total.astype(jnp.bfloat16)


def input_kernel(
    blocks_ref, others_ref, rows_ref, dlogits_ref, head_ref, input_ref, weight_ref, other_ref, held_ref, sems
):
    positions, piles, channels = rows_ref.shape
    assemble(blocks_ref, weight_ref)
    assemble(others_ref, other_ref)
    dlogits = [dlogits_ref[:, kind : kind + 1] for kind in range(head_ref.shape[0])]
    dpres = []
    for half, half_ref in ((core_index(), weight_ref), (1 - core_index(), other_ref)):
        slope = gelu_parts(product(rows_ref, half_ref))[1]
        dpres.append((spread(dlogits, head_half(head_ref, half), positions) * slope).astype(jnp.bfloat16))
    wide = channels // X
    copies = []
    for x in range(X):
        span = pl.ds(x * wide, wide)
        back = jnp.dot(dpres[0], weight_ref[:, span], preferred_element_type=jnp.float32)
        back = back + jnp.dot(dpres[1], other_ref[:, span], preferred_element_type=jnp.float32)
        held_ref[:, :, span] = back.astype(jnp.bfloat16).reshape(positions, piles, wide)
        copies.append(
            pltpu.make_async_copy(held_ref.at[:, :, span], input_ref.at[:, :, span], sems.at[x])
        )
        copies[-1].start()
    for copy in copies:
        copy.wait()


def adam_kernel(
    own_ref, other_ref, weight_ref, first_ref, second_ref, out_weight, out_first, out_second, flip_ref
):
    half = own_ref.shape[0]
    core = core_index()
    flip_ref[pl.ds(pl.multiple_of(core * half, half), half), :] = own_ref[...]
    flip_ref[pl.ds(pl.multiple_of((1 - core) * half, half), half), :] = other_ref[...]
    grad = flip_ref[...].T
    new_first = beta_one * first_ref[...] + (1.0 - beta_one) * grad
    new_second = beta_two * second_ref[...] + (1.0 - beta_two) * grad * grad
    first_hat = new_first / (1.0 - beta_one**bias_steps)
    second_hat = new_second / (1.0 - beta_two**bias_steps)
    out_weight[...] = weight_ref[...] - learn_rate * first_hat / (jnp.sqrt(second_hat) + epsilon)
    out_first[...] = new_first
    out_second[...] = new_second


def per_device(features, labels, weight, head, moment_one, moment_two):
    piles, positions, channels = features.shape
    shard, outputs = weight.shape
    count = piles * positions
    half_outs = outputs // 2
    deep = half_outs // PAIR
    rows = features.transpose(1, 0, 2)
    flat_head = head.T
    vmem = pl.BlockSpec(memory_space=pltpu.VMEM)
    anywhere = pl.BlockSpec(memory_space=pl.ANY)
    params = pltpu.CompilerParams(vmem_limit_bytes=16 << 20)

    half = pl.pallas_call(
        prepare_kernel,
        out_shape=jax.ShapeDtypeStruct((half_outs, shard), jnp.bfloat16),
        in_specs=[vmem],
        out_specs=vmem,
        scratch_shapes=[pltpu.VMEM((outputs, shard), jnp.float32)],
        compiler_params=params,
        name="prepare",
    )(weight)
    pair = jnp.stack([half, lax.ppermute(half, AXES, CROSS)])
    sent_rows, pair = lax.optimization_barrier((rows, pair))
    other_rows = swap_cores(sent_rows)
    copies = jnp.broadcast_to(pair, (X * PAIR, PAIR, half_outs, shard))
    blocks = exchange(copies, OVER_XY).reshape(GROUP, half_outs, shard)

    flops = 2 * count * channels * outputs
    slope, logits = pl.pallas_call(
        forward_kernel,
        out_shape=(
            jax.ShapeDtypeStruct((CORE, count, half_outs), jnp.float32),
            jax.ShapeDtypeStruct((CORE, piles, 128), jnp.float32),
        ),
        in_specs=[vmem] * 5,
        out_specs=(vmem,) * 2,
        scratch_shapes=[pltpu.VMEM((half_outs, channels), jnp.bfloat16)],
        compiler_params=params,
        cost_estimate=pl.CostEstimate(
            flops=flops, bytes_accessed=4 << 20, transcendentals=count * outputs
        ),
        name="forward",
    )(blocks, rows, other_rows, labels.reshape(1, piles), flat_head)

    received = swap_cores(logits)
    grad, dlogits = pl.pallas_call(
        gradient_kernel,
        out_shape=(
            jax.ShapeDtypeStruct((X, PAIR, PAIR, YL // PAIR, deep, shard), jnp.bfloat16),
            jax.ShapeDtypeStruct((piles, 128), jnp.float32),
        ),
        in_specs=[vmem] * 6,
        out_specs=(vmem,) * 2,
        compiler_params=params,
        cost_estimate=pl.CostEstimate(flops=flops, bytes_accessed=4 << 20, transcendentals=0),
        name="gradient",
    )(logits, received, slope, rows, other_rows, flat_head)

    both = grad.reshape(GROUP, -1, deep, shard)
    parts = exchange(both, OVER_XYZ)
    other_blocks = swap_cores(blocks)
    input_grad = pl.pallas_call(
        input_kernel,
        out_shape=jax.ShapeDtypeStruct((positions, piles, channels), jnp.bfloat16),
        in_specs=[vmem] * 5,
        out_specs=anywhere,
        scratch_shapes=[
            pltpu.VMEM((half_outs, channels), jnp.bfloat16),
            pltpu.VMEM((half_outs, channels), jnp.bfloat16),
            pltpu.VMEM((positions, piles, channels), jnp.bfloat16),
            pltpu.SemaphoreType.DMA((X,)),
        ],
        compiler_params=params,
        cost_estimate=pl.CostEstimate(
            flops=flops, bytes_accessed=4 << 20, transcendentals=count * outputs
        ),
        name="input_grad",
    )(blocks, other_blocks, rows, dlogits, flat_head)
    parts, input_grad = lax.optimization_barrier((parts, input_grad))
    copies = pl.pallas_call(
        sum_kernel,
        out_shape=jax.ShapeDtypeStruct((YH * parts.shape[1], deep, shard), jnp.bfloat16),
        in_specs=[vmem],
        out_specs=vmem,
        compiler_params=params,
        name="sum",
    )(parts)
    over_y = jnp.sum(exchange(copies, OVER_Y).astype(jnp.float32), axis=0).astype(jnp.bfloat16)
    parts = exchange(jnp.broadcast_to(over_y, (Z, deep, shard)), OVER_Z)
    mine = jnp.sum(parts.reshape(PAIR, Z // PAIR, deep, shard).astype(jnp.float32), axis=1)
    mine = mine.reshape(half_outs, shard)

    theirs = swap_cores(mine)
    new_weight, new_first, new_second = pl.pallas_call(
        adam_kernel,
        out_shape=(jax.ShapeDtypeStruct((shard, outputs), jnp.float32),) * 3,
        in_specs=[vmem] * 5,
        out_specs=(vmem,) * 3,
        scratch_shapes=[pltpu.VMEM((outputs, shard), jnp.float32)],
        compiler_params=params,
        name="adam",
    )(mine, theirs, weight, moment_one, moment_two)
    return (input_grad.transpose(1, 0, 2), new_weight, new_first, new_second)


def solution(mesh):
    return jax.shard_map(
        per_device,
        mesh=mesh,
        in_specs=(
            P(("dp", "group"), None, None),
            P(("dp", "group")),
            P("group", None),
            P(),
            P("group", None),
            P("group", None),
        ),
        out_specs=(
            P(("dp", "group"), None, None),
            P("group", None),
            P("group", None),
            P("group", None),
        ),
        check_vma=False,
    )
```

```python
import functools
import math

import jax
import jax.numpy as jnp
from jax import lax
from jax.experimental import pallas as pl
from jax.experimental.pallas import tpu as pltpu
from jax.sharding import PartitionSpec as P

beta_one = 0.9
beta_two = 0.999
learn_rate = 0.01
epsilon = 1e-08
bias_steps = 10.0

AXES = ("dp", "group")
Z, YH, CORE, X, YL = 8, 2, 2, 4, 4
GROUP = X * YL
PAIR = 2
root = math.sqrt(2.0 / math.pi)
cubic = 0.044715


def index(z, yh, c, x, yl):
    return ((z * YH + yh) * CORE + c) * GROUP + x * YL + yl


def places():
    for z in range(Z):
        for yh in range(YH):
            for c in range(CORE):
                for x in range(X):
                    for yl in range(YL):
                        yield z, yh, c, x, yl


def groups(key, order):
    held = {}
    for place in places():
        held.setdefault(key(*place), []).append((order(*place), index(*place)))
    return [[at for _, at in sorted(held[name])] for name in sorted(held)]


def pair_of(y, c):
    return (y - c) % (YH * YL) // PAIR


def beyond(yh, yl, c):
    at = (yh * YL + yl + (1 if (yl + c) % PAIR else -1)) % (YH * YL)
    return at // YL, at % YL


OVER_XY = groups(
    lambda z, yh, c, x, yl: (z, c, pair_of(yh * YL + yl, c)), lambda z, yh, c, x, yl: (x, yl % PAIR)
)
OVER_XYZ = groups(
    lambda z, yh, c, x, yl: (z // PAIR, yh, c, yl // PAIR), lambda z, yh, c, x, yl: (x, yl % PAIR, z % PAIR)
)
OVER_Y = groups(lambda z, yh, c, x, yl: (z, c, x, yl % PAIR), lambda z, yh, c, x, yl: (yh, yl))
OVER_Z = groups(lambda z, yh, c, x, yl: (yh, c, x, yl), lambda z, yh, c, x, yl: (z % PAIR, z))
SWAP = [(index(z, yh, c, x, yl), index(z, yh, 1 - c, x, yl)) for z, yh, c, x, yl in places()]


CROSS = [
    (index(z, yh, c, x, yl), index(z, beyond(yh, yl, c)[0], c, x, beyond(yh, yl, c)[1]))
    for z, yh, c, x, yl in places()
]


def swap_cores(value):
    return lax.ppermute(value, AXES, SWAP)


def exchange(value, members):
    return lax.all_to_all(value, AXES, 0, 0, tiled=True, axis_index_groups=members)


def core_index():
    return lax.rem(lax.axis_index("dp"), CORE)


def gelu_parts(pre):
    square = pre * pre
    bend = jnp.tanh(root * (pre + cubic * (pre * square)))
    act = 0.5 * pre * (1.0 + bend)
    slope = 0.5 * (1.0 + bend) + 0.5 * pre * (1.0 - bend * bend) * (root * (1.0 + 3.0 * cubic * square))
    return act, slope


def product(rows_ref, weight_ref):
    positions, piles, channels = rows_ref.shape
    return lax.dot_general(
        rows_ref[...].reshape(positions * piles, channels),
        weight_ref[...],
        (((1,), (1,)), ((), ())),
        preferred_element_type=jnp.float32,
    )


def head_half(head_ref, half):
    count = head_ref.shape[1] // 2
    whole = head_ref[...]
    chosen = jnp.where(half == 0, whole[:, :count], whole[:, count:])
    return [chosen[kind : kind + 1, :] for kind in range(head_ref.shape[0])]


def in_lanes(columns):
    lane = lax.broadcasted_iota(jnp.int32, (columns[0].shape[0], 128), 1)
    held = jnp.zeros(lane.shape, jnp.float32)
    for at, column in enumerate(columns):
        held = jnp.where(lane == at, column, held)
    return held


def spread(dlogits, heads, positions):
    dpooled = functools.reduce(jnp.add, [column * vector for column, vector in zip(dlogits, heads)])
    return jnp.concatenate([dpooled / positions] * positions, axis=0)


def prepare_kernel(weight_ref, out_ref, flip_ref):
    half = out_ref.shape[0]
    flip_ref[...] = weight_ref[...].T
    out_ref[...] = flip_ref[pl.ds(pl.multiple_of(core_index() * half, half), half), :].astype(jnp.bfloat16)


def shards_of(core, far):
    yl = lax.rem(lax.axis_index("group"), YL)
    odd = lax.rem(yl, PAIR)
    step = 1 - 2 * core
    even_at = lax.rem(yl - odd * step + YL, YL)
    odd_at = lax.rem(yl + (1 - odd) * step + YL, YL)
    return [x * YL + lax.rem(at + PAIR * far, YL) for x in range(X) for at in (even_at, odd_at)]


def assemble(core, near_ref, far_ref, weight_ref):
    width = near_ref.shape[2]
    for far, blocks_ref in enumerate((near_ref, far_ref)):
        for block, shard in enumerate(shards_of(core, far)):
            weight_ref[:, pl.ds(pl.multiple_of(shard * width, width), width)] = blocks_ref[block]


def channels_of(side, span):
    return jnp.concatenate(
        [ref[at, :, span] for ref in side for at in range(ref.shape[0])], axis=0
    )


def partial_product(core, far, blocks_ref, side):
    width = blocks_ref.shape[2]
    shards = shards_of(core, far)
    total = None
    for block in range(0, len(shards), 2):
        spans = [pl.ds(pl.multiple_of(shard * width, width), width) for shard in shards[block : block + 2]]
        part = lax.dot_general(
            jnp.concatenate([channels_of(side, span) for span in spans], axis=1),
            jnp.concatenate([blocks_ref[block], blocks_ref[block + 1]], axis=1),
            (((1,), (1,)), ((), ())),
            preferred_element_type=jnp.float32,
        )
        total = part if total is None else total + part
    return total


def near_kernel(blocks_ref, rows_ref, first_ref, last_ref, pre_ref):
    for at, side in enumerate(((rows_ref,), (first_ref, last_ref))):
        pre_ref[at] = partial_product(core_index(), 0, blocks_ref, side)


def forward_kernel(
    pre_ref, blocks_ref, rows_ref, first_ref, last_ref, labels_ref, head_ref, slope_ref, logits_ref
):
    positions, piles, channels = rows_ref.shape
    heads = head_half(head_ref, core_index())
    across = lax.broadcasted_iota(jnp.int32, (piles, piles), 0) == lax.broadcasted_iota(
        jnp.int32, (piles, piles), 1
    )
    marks = jnp.sum(
        jnp.where(across, labels_ref[...].astype(jnp.float32), 0.0), axis=1, keepdims=True
    )
    for side, refs in enumerate(((rows_ref,), (first_ref, last_ref))):
        pre = pre_ref[side] + partial_product(core_index(), 1, blocks_ref, refs)
        act, slope = gelu_parts(pre)
        slope_ref[side] = slope
        pooled = functools.reduce(
            jnp.add, [act[position * piles : (position + 1) * piles] for position in range(positions)]
        )
        pooled = pooled / positions
        logits = [jnp.sum(pooled * vector, axis=1, keepdims=True) for vector in heads]
        logits_ref[side] = in_lanes(logits + [marks] if side == 0 else logits)


def gradient_kernel(
    logits_ref, received_ref, slope_ref, rows_ref, first_ref, last_ref, head_ref, grad_ref, dlogits_ref
):
    positions, piles, channels = rows_ref.shape
    classes = head_ref.shape[0]
    heads = head_half(head_ref, core_index())
    lefts = []
    for side in range(CORE):
        mine, theirs = logits_ref[side], received_ref[1 - side]
        marks = (mine if side == 0 else theirs)[:, classes : classes + 1]
        logits = [mine[:, kind : kind + 1] + theirs[:, kind : kind + 1] for kind in range(classes)]
        top = functools.reduce(jnp.maximum, logits)
        powers = [jnp.exp(value - top) for value in logits]
        total = functools.reduce(jnp.add, powers)
        dlogits = [
            powers[kind] / total - jnp.where(marks == float(kind), 1.0, 0.0) for kind in range(classes)
        ]
        dpre = spread(dlogits, heads, positions) * slope_ref[side]
        if side == 0:
            dlogits_ref[...] = in_lanes(dlogits)
        lefts.append(dpre.T.astype(jnp.bfloat16))
    wide = channels // X
    width = wide // YL
    deep = lefts[0].shape[0] // PAIR
    for x in range(X):
        parts = [
            jnp.dot(
                left,
                channels_of(refs, slice(x * wide, (x + 1) * wide)),
                preferred_element_type=jnp.float32,
            )
            for left, refs in zip(lefts, ((rows_ref,), (first_ref, last_ref)))
        ]
        total = (parts[0] + parts[1]).astype(jnp.bfloat16)
        for part in range(PAIR):
            for yl in range(YL):
                grad_ref[x, yl % PAIR, part, yl // PAIR] = total[
                    part * deep : (part + 1) * deep, yl * width : (yl + 1) * width
                ]


def sum_kernel(parts_ref, out_ref):
    count, rows = parts_ref.shape[:2]
    total = parts_ref[0].astype(jnp.float32)
    for at in range(1, count):
        total = total + parts_ref[at].astype(jnp.float32)
    for copy in range(out_ref.shape[0] // rows):
        out_ref[copy * rows : (copy + 1) * rows] = total.astype(jnp.bfloat16)


def input_kernel(
    near_ref, far_ref, near_other_ref, far_other_ref, rows_ref, dlogits_ref, head_ref, input_ref,
    weight_ref, other_ref, held_ref, sems
):
    positions, piles, channels = rows_ref.shape
    assemble(core_index(), near_ref, far_ref, weight_ref)
    assemble(1 - core_index(), near_other_ref, far_other_ref, other_ref)
    dlogits = [dlogits_ref[:, kind : kind + 1] for kind in range(head_ref.shape[0])]
    dpres = []
    for half, half_ref in ((core_index(), weight_ref), (1 - core_index(), other_ref)):
        slope = gelu_parts(product(rows_ref, half_ref))[1]
        dpres.append((spread(dlogits, head_half(head_ref, half), positions) * slope).astype(jnp.bfloat16))
    wide = channels // X
    copies = []
    for x in range(X):
        span = pl.ds(x * wide, wide)
        back = jnp.dot(dpres[0], weight_ref[:, span], preferred_element_type=jnp.float32)
        back = back + jnp.dot(dpres[1], other_ref[:, span], preferred_element_type=jnp.float32)
        held_ref[:, :, span] = back.astype(jnp.bfloat16).reshape(positions, piles, wide)
        copies.append(
            pltpu.make_async_copy(held_ref.at[:, :, span], input_ref.at[:, :, span], sems.at[x])
        )
        copies[-1].start()
    for copy in copies:
        copy.wait()


def adam_kernel(
    own_ref, other_ref, weight_ref, first_ref, second_ref, out_weight, out_first, out_second, flip_ref
):
    half = own_ref.shape[0]
    core = core_index()
    flip_ref[pl.ds(pl.multiple_of(core * half, half), half), :] = own_ref[...]
    flip_ref[pl.ds(pl.multiple_of((1 - core) * half, half), half), :] = other_ref[...]
    grad = flip_ref[...].T
    new_first = beta_one * first_ref[...] + (1.0 - beta_one) * grad
    new_second = beta_two * second_ref[...] + (1.0 - beta_two) * grad * grad
    first_hat = new_first / (1.0 - beta_one**bias_steps)
    second_hat = new_second / (1.0 - beta_two**bias_steps)
    out_weight[...] = weight_ref[...] - learn_rate * first_hat / (jnp.sqrt(second_hat) + epsilon)
    out_first[...] = new_first
    out_second[...] = new_second


def per_device(features, labels, weight, head, moment_one, moment_two):
    piles, positions, channels = features.shape
    shard, outputs = weight.shape
    count = piles * positions
    half_outs = outputs // 2
    deep = half_outs // PAIR
    rows = features.transpose(1, 0, 2)
    flat_head = head.T
    vmem = pl.BlockSpec(memory_space=pltpu.VMEM)
    anywhere = pl.BlockSpec(memory_space=pl.ANY)
    params = pltpu.CompilerParams(vmem_limit_bytes=16 << 20)

    half = pl.pallas_call(
        prepare_kernel,
        out_shape=jax.ShapeDtypeStruct((half_outs, shard), jnp.bfloat16),
        in_specs=[vmem],
        out_specs=vmem,
        scratch_shapes=[pltpu.VMEM((outputs, shard), jnp.float32)],
        compiler_params=params,
        name="prepare",
    )(weight)
    sent_rows, half = lax.optimization_barrier((rows, half))
    other_rows = (swap_cores(sent_rows[:2]), swap_cores(sent_rows[2:]))
    near = exchange(jnp.broadcast_to(half, (X * PAIR, half_outs, shard)), OVER_XY)
    far = lax.ppermute(near, AXES, CROSS)

    flops = 2 * count * channels * outputs
    pre = pl.pallas_call(
        near_kernel,
        out_shape=jax.ShapeDtypeStruct((CORE, count, half_outs), jnp.float32),
        in_specs=[vmem] * 4,
        out_specs=vmem,
        compiler_params=params,
        cost_estimate=pl.CostEstimate(flops=flops // 2, bytes_accessed=4 << 20, transcendentals=0),
        name="forward_near",
    )(near, rows, *other_rows)
    slope, logits = pl.pallas_call(
        forward_kernel,
        out_shape=(
            jax.ShapeDtypeStruct((CORE, count, half_outs), jnp.float32),
            jax.ShapeDtypeStruct((CORE, piles, 128), jnp.float32),
        ),
        in_specs=[vmem] * 7,
        out_specs=(vmem,) * 2,
        compiler_params=params,
        cost_estimate=pl.CostEstimate(
            flops=flops // 2, bytes_accessed=4 << 20, transcendentals=count * outputs
        ),
        name="forward_far",
    )(pre, far, rows, *other_rows, labels.reshape(1, piles), flat_head)

    received = swap_cores(logits)
    grad, dlogits = pl.pallas_call(
        gradient_kernel,
        out_shape=(
            jax.ShapeDtypeStruct((X, PAIR, PAIR, YL // PAIR, deep, shard), jnp.bfloat16),
            jax.ShapeDtypeStruct((piles, 128), jnp.float32),
        ),
        in_specs=[vmem] * 7,
        out_specs=(vmem,) * 2,
        compiler_params=params,
        cost_estimate=pl.CostEstimate(flops=flops, bytes_accessed=4 << 20, transcendentals=0),
        name="gradient",
    )(logits, received, slope, rows, *other_rows, flat_head)

    both = grad.reshape(GROUP, -1, deep, shard)
    parts = exchange(both, OVER_XYZ)
    near_other, far_other = swap_cores(near), swap_cores(far)
    input_grad = pl.pallas_call(
        input_kernel,
        out_shape=jax.ShapeDtypeStruct((positions, piles, channels), jnp.bfloat16),
        in_specs=[vmem] * 7,
        out_specs=anywhere,
        scratch_shapes=[
            pltpu.VMEM((half_outs, channels), jnp.bfloat16),
            pltpu.VMEM((half_outs, channels), jnp.bfloat16),
            pltpu.VMEM((positions, piles, channels), jnp.bfloat16),
            pltpu.SemaphoreType.DMA((X,)),
        ],
        compiler_params=params,
        cost_estimate=pl.CostEstimate(
            flops=flops, bytes_accessed=4 << 20, transcendentals=count * outputs
        ),
        name="input_grad",
    )(near, far, near_other, far_other, rows, dlogits, flat_head)
    parts, input_grad = lax.optimization_barrier((parts, input_grad))
    copies = pl.pallas_call(
        sum_kernel,
        out_shape=jax.ShapeDtypeStruct((YH * parts.shape[1], deep, shard), jnp.bfloat16),
        in_specs=[vmem],
        out_specs=vmem,
        compiler_params=params,
        name="sum",
    )(parts)
    over_y = jnp.sum(exchange(copies, OVER_Y).astype(jnp.float32), axis=0).astype(jnp.bfloat16)
    parts = exchange(jnp.broadcast_to(over_y, (Z, deep, shard)), OVER_Z)
    mine = jnp.sum(parts.reshape(PAIR, Z // PAIR, deep, shard).astype(jnp.float32), axis=1)
    mine = mine.reshape(half_outs, shard)

    theirs = swap_cores(mine)
    new_weight, new_first, new_second = pl.pallas_call(
        adam_kernel,
        out_shape=(jax.ShapeDtypeStruct((shard, outputs), jnp.float32),) * 3,
        in_specs=[vmem] * 5,
        out_specs=(vmem,) * 3,
        scratch_shapes=[pltpu.VMEM((outputs, shard), jnp.float32)],
        compiler_params=params,
        name="adam",
    )(mine, theirs, weight, moment_one, moment_two)
    return (input_grad.transpose(1, 0, 2), new_weight, new_first, new_second)


def solution(mesh):
    return jax.shard_map(
        per_device,
        mesh=mesh,
        in_specs=(
            P(("dp", "group"), None, None),
            P(("dp", "group")),
            P("group", None),
            P(),
            P("group", None),
            P("group", None),
        ),
        out_specs=(
            P(("dp", "group"), None, None),
            P("group", None),
            P("group", None),
            P("group", None),
        ),
        check_vma=False,
    )
```

```python
import functools
import math

import jax
import jax.numpy as jnp
from jax import lax
from jax.experimental import pallas as pl
from jax.experimental.pallas import tpu as pltpu
from jax.sharding import PartitionSpec as P

beta_one = 0.9
beta_two = 0.999
learn_rate = 0.01
epsilon = 1e-08
bias_steps = 10.0

AXES = ("dp", "group")
Z, YH, CORE, X, YL = 8, 2, 2, 4, 4
GROUP = X * YL
PAIR = 2
root = math.sqrt(2.0 / math.pi)
cubic = 0.044715


def index(z, yh, c, x, yl):
    return ((z * YH + yh) * CORE + c) * GROUP + x * YL + yl


def places():
    for z in range(Z):
        for yh in range(YH):
            for c in range(CORE):
                for x in range(X):
                    for yl in range(YL):
                        yield z, yh, c, x, yl


def groups(key, order):
    held = {}
    for place in places():
        held.setdefault(key(*place), []).append((order(*place), index(*place)))
    return [[at for _, at in sorted(held[name])] for name in sorted(held)]


def pair_of(y, c):
    return (y - 1 + c) % (YH * YL) // PAIR


def beyond(yh, yl, c):
    at = (yh * YL + yl + (-1 if (yl + c) % PAIR else 1)) % (YH * YL)
    return at // YL, at % YL


OVER_XY = groups(
    lambda z, yh, c, x, yl: (z, c, pair_of(yh * YL + yl, c)), lambda z, yh, c, x, yl: (x, yl % PAIR)
)
OVER_XYZ = groups(
    lambda z, yh, c, x, yl: (z // PAIR, yh, c, yl // PAIR), lambda z, yh, c, x, yl: (x, yl % PAIR, z % PAIR)
)
OVER_Y = groups(lambda z, yh, c, x, yl: (z, c, x, yl % PAIR), lambda z, yh, c, x, yl: (yh, yl))
OVER_Z = groups(lambda z, yh, c, x, yl: (yh, c, x, yl), lambda z, yh, c, x, yl: (z % PAIR, z))
SWAP = [(index(z, yh, c, x, yl), index(z, yh, 1 - c, x, yl)) for z, yh, c, x, yl in places()]


CROSS = [
    (index(z, yh, c, x, yl), index(z, beyond(yh, yl, c)[0], c, x, beyond(yh, yl, c)[1]))
    for z, yh, c, x, yl in places()
]


def swap_cores(value):
    return lax.ppermute(value, AXES, SWAP)


def exchange(value, members):
    return lax.all_to_all(value, AXES, 0, 0, tiled=True, axis_index_groups=members)


def core_index():
    return lax.rem(lax.axis_index("dp"), CORE)


def gelu_parts(pre):
    square = pre * pre
    bend = jnp.tanh(root * (pre + cubic * (pre * square)))
    act = 0.5 * pre * (1.0 + bend)
    slope = 0.5 * (1.0 + bend) + 0.5 * pre * (1.0 - bend * bend) * (root * (1.0 + 3.0 * cubic * square))
    return act, slope


def product(rows_ref, weight_ref):
    positions, piles, channels = rows_ref.shape
    return lax.dot_general(
        rows_ref[...].reshape(positions * piles, channels),
        weight_ref[...],
        (((1,), (1,)), ((), ())),
        preferred_element_type=jnp.float32,
    )


def head_half(head_ref, half):
    count = head_ref.shape[1] // 2
    whole = head_ref[...]
    chosen = jnp.where(half == 0, whole[:, :count], whole[:, count:])
    return [chosen[kind : kind + 1, :] for kind in range(head_ref.shape[0])]


def in_lanes(columns):
    lane = lax.broadcasted_iota(jnp.int32, (columns[0].shape[0], 128), 1)
    held = jnp.zeros(lane.shape, jnp.float32)
    for at, column in enumerate(columns):
        held = jnp.where(lane == at, column, held)
    return held


def spread(dlogits, heads, positions):
    dpooled = functools.reduce(jnp.add, [column * vector for column, vector in zip(dlogits, heads)])
    return jnp.concatenate([dpooled / positions] * positions, axis=0)


def prepare_kernel(weight_ref, out_ref, flip_ref):
    half = out_ref.shape[0]
    flip_ref[...] = weight_ref[...].T
    out_ref[...] = flip_ref[pl.ds(pl.multiple_of(core_index() * half, half), half), :].astype(jnp.bfloat16)


def shards_of(core, far):
    yl = lax.rem(lax.axis_index("group"), YL)
    odd = lax.rem(yl, PAIR)
    step = 2 * core - 1
    even_at = lax.rem(yl - odd * step + YL, YL)
    odd_at = lax.rem(yl + (1 - odd) * step + YL, YL)
    return [x * YL + lax.rem(at + PAIR * far, YL) for x in range(X) for at in (even_at, odd_at)]


def assemble(core, near_ref, far_ref, weight_ref):
    width = near_ref.shape[2]
    for far, blocks_ref in enumerate((near_ref, far_ref)):
        for block, shard in enumerate(shards_of(core, far)):
            weight_ref[:, pl.ds(pl.multiple_of(shard * width, width), width)] = blocks_ref[block]


def channels_of(side, span):
    return jnp.concatenate(
        [ref[at, :, span] for ref in side for at in range(ref.shape[0])], axis=0
    )


def partial_product(core, far, blocks_ref, side):
    width = blocks_ref.shape[2]
    shards = shards_of(core, far)
    total = None
    for block in range(0, len(shards), 2):
        spans = [pl.ds(pl.multiple_of(shard * width, width), width) for shard in shards[block : block + 2]]
        part = lax.dot_general(
            jnp.concatenate([channels_of(side, span) for span in spans], axis=1),
            jnp.concatenate([blocks_ref[block], blocks_ref[block + 1]], axis=1),
            (((1,), (1,)), ((), ())),
            preferred_element_type=jnp.float32,
        )
        total = part if total is None else total + part
    return total


def near_kernel(blocks_ref, rows_ref, first_ref, last_ref, pre_ref):
    for at, side in enumerate(((rows_ref,), (first_ref, last_ref))):
        pre_ref[at] = partial_product(core_index(), 0, blocks_ref, side)


def forward_kernel(
    pre_ref, blocks_ref, rows_ref, first_ref, last_ref, labels_ref, head_ref, slope_ref, logits_ref
):
    positions, piles, channels = rows_ref.shape
    heads = head_half(head_ref, core_index())
    across = lax.broadcasted_iota(jnp.int32, (piles, piles), 0) == lax.broadcasted_iota(
        jnp.int32, (piles, piles), 1
    )
    marks = jnp.sum(
        jnp.where(across, labels_ref[...].astype(jnp.float32), 0.0), axis=1, keepdims=True
    )
    for side, refs in enumerate(((rows_ref,), (first_ref, last_ref))):
        pre = pre_ref[side] + partial_product(core_index(), 1, blocks_ref, refs)
        act, slope = gelu_parts(pre)
        slope_ref[side] = slope
        pooled = functools.reduce(
            jnp.add, [act[position * piles : (position + 1) * piles] for position in range(positions)]
        )
        pooled = pooled / positions
        logits = [jnp.sum(pooled * vector, axis=1, keepdims=True) for vector in heads]
        logits_ref[side] = in_lanes(logits + [marks] if side == 0 else logits)


def gradient_kernel(
    logits_ref, received_ref, slope_ref, rows_ref, first_ref, last_ref, head_ref, grad_ref, dlogits_ref
):
    positions, piles, channels = rows_ref.shape
    classes = head_ref.shape[0]
    heads = head_half(head_ref, core_index())
    lefts = []
    for side in range(CORE):
        mine, theirs = logits_ref[side], received_ref[1 - side]
        marks = (mine if side == 0 else theirs)[:, classes : classes + 1]
        logits = [mine[:, kind : kind + 1] + theirs[:, kind : kind + 1] for kind in range(classes)]
        top = functools.reduce(jnp.maximum, logits)
        powers = [jnp.exp(value - top) for value in logits]
        total = functools.reduce(jnp.add, powers)
        dlogits = [
            powers[kind] / total - jnp.where(marks == float(kind), 1.0, 0.0) for kind in range(classes)
        ]
        dpre = spread(dlogits, heads, positions) * slope_ref[side]
        if side == 0:
            dlogits_ref[...] = in_lanes(dlogits)
        lefts.append(dpre.T.astype(jnp.bfloat16))
    wide = channels // X
    width = wide // YL
    deep = lefts[0].shape[0] // PAIR
    for x in range(X):
        parts = [
            jnp.dot(
                left,
                channels_of(refs, slice(x * wide, (x + 1) * wide)),
                preferred_element_type=jnp.float32,
            )
            for left, refs in zip(lefts, ((rows_ref,), (first_ref, last_ref)))
        ]
        total = (parts[0] + parts[1]).astype(jnp.bfloat16)
        for part in range(PAIR):
            for yl in range(YL):
                grad_ref[x, yl % PAIR, part, yl // PAIR] = total[
                    part * deep : (part + 1) * deep, yl * width : (yl + 1) * width
                ]


def sum_kernel(parts_ref, out_ref):
    count, rows = parts_ref.shape[:2]
    total = parts_ref[0].astype(jnp.float32)
    for at in range(1, count):
        total = total + parts_ref[at].astype(jnp.float32)
    for copy in range(out_ref.shape[0] // rows):
        out_ref[copy * rows : (copy + 1) * rows] = total.astype(jnp.bfloat16)


def input_kernel(
    near_ref, far_ref, near_other_ref, far_other_ref, rows_ref, dlogits_ref, head_ref, input_ref,
    weight_ref, other_ref, held_ref, sems
):
    positions, piles, channels = rows_ref.shape
    assemble(core_index(), near_ref, far_ref, weight_ref)
    assemble(1 - core_index(), near_other_ref, far_other_ref, other_ref)
    dlogits = [dlogits_ref[:, kind : kind + 1] for kind in range(head_ref.shape[0])]
    dpres = []
    for half, half_ref in ((core_index(), weight_ref), (1 - core_index(), other_ref)):
        slope = gelu_parts(product(rows_ref, half_ref))[1]
        dpres.append((spread(dlogits, head_half(head_ref, half), positions) * slope).astype(jnp.bfloat16))
    wide = channels // X
    copies = []
    for x in range(X):
        span = pl.ds(x * wide, wide)
        back = jnp.dot(dpres[0], weight_ref[:, span], preferred_element_type=jnp.float32)
        back = back + jnp.dot(dpres[1], other_ref[:, span], preferred_element_type=jnp.float32)
        held_ref[:, :, span] = back.astype(jnp.bfloat16).reshape(positions, piles, wide)
        copies.append(
            pltpu.make_async_copy(held_ref.at[:, :, span], input_ref.at[:, :, span], sems.at[x])
        )
        copies[-1].start()
    for copy in copies:
        copy.wait()


def adam_kernel(
    own_ref, other_ref, weight_ref, first_ref, second_ref, out_weight, out_first, out_second, flip_ref
):
    half = own_ref.shape[0]
    core = core_index()
    flip_ref[pl.ds(pl.multiple_of(core * half, half), half), :] = own_ref[...]
    flip_ref[pl.ds(pl.multiple_of((1 - core) * half, half), half), :] = other_ref[...]
    grad = flip_ref[...].T
    new_first = beta_one * first_ref[...] + (1.0 - beta_one) * grad
    new_second = beta_two * second_ref[...] + (1.0 - beta_two) * grad * grad
    first_hat = new_first / (1.0 - beta_one**bias_steps)
    second_hat = new_second / (1.0 - beta_two**bias_steps)
    out_weight[...] = weight_ref[...] - learn_rate * first_hat / (jnp.sqrt(second_hat) + epsilon)
    out_first[...] = new_first
    out_second[...] = new_second


def per_device(features, labels, weight, head, moment_one, moment_two):
    piles, positions, channels = features.shape
    shard, outputs = weight.shape
    count = piles * positions
    half_outs = outputs // 2
    deep = half_outs // PAIR
    rows = features.transpose(1, 0, 2)
    flat_head = head.T
    vmem = pl.BlockSpec(memory_space=pltpu.VMEM)
    anywhere = pl.BlockSpec(memory_space=pl.ANY)
    params = pltpu.CompilerParams(vmem_limit_bytes=16 << 20)

    half = pl.pallas_call(
        prepare_kernel,
        out_shape=jax.ShapeDtypeStruct((half_outs, shard), jnp.bfloat16),
        in_specs=[vmem],
        out_specs=vmem,
        scratch_shapes=[pltpu.VMEM((outputs, shard), jnp.float32)],
        compiler_params=params,
        name="prepare",
    )(weight)
    sent_rows, half = lax.optimization_barrier((rows, half))
    near = exchange(jnp.broadcast_to(half, (X * PAIR, half_outs, shard)), OVER_XY)
    later_rows, near = lax.optimization_barrier((rows, near))
    other_rows = (swap_cores(sent_rows[:4]), swap_cores(later_rows[4:]))
    far = lax.ppermute(near, AXES, CROSS)

    flops = 2 * count * channels * outputs
    pre = pl.pallas_call(
        near_kernel,
        out_shape=jax.ShapeDtypeStruct((CORE, count, half_outs), jnp.float32),
        in_specs=[vmem] * 4,
        out_specs=vmem,
        compiler_params=params,
        cost_estimate=pl.CostEstimate(flops=flops // 2, bytes_accessed=4 << 20, transcendentals=0),
        name="forward_near",
    )(near, rows, *other_rows)
    slope, logits = pl.pallas_call(
        forward_kernel,
        out_shape=(
            jax.ShapeDtypeStruct((CORE, count, half_outs), jnp.float32),
            jax.ShapeDtypeStruct((CORE, piles, 128), jnp.float32),
        ),
        in_specs=[vmem] * 7,
        out_specs=(vmem,) * 2,
        compiler_params=params,
        cost_estimate=pl.CostEstimate(
            flops=flops // 2, bytes_accessed=4 << 20, transcendentals=count * outputs
        ),
        name="forward_far",
    )(pre, far, rows, *other_rows, labels.reshape(1, piles), flat_head)

    received = swap_cores(logits)
    grad, dlogits = pl.pallas_call(
        gradient_kernel,
        out_shape=(
            jax.ShapeDtypeStruct((X, PAIR, PAIR, YL // PAIR, deep, shard), jnp.bfloat16),
            jax.ShapeDtypeStruct((piles, 128), jnp.float32),
        ),
        in_specs=[vmem] * 7,
        out_specs=(vmem,) * 2,
        compiler_params=params,
        cost_estimate=pl.CostEstimate(flops=flops, bytes_accessed=4 << 20, transcendentals=0),
        name="gradient",
    )(logits, received, slope, rows, *other_rows, flat_head)

    both = grad.reshape(GROUP, -1, deep, shard)
    parts = exchange(both, OVER_XYZ)
    near_other, far_other = swap_cores(near), swap_cores(far)
    input_grad = pl.pallas_call(
        input_kernel,
        out_shape=jax.ShapeDtypeStruct((positions, piles, channels), jnp.bfloat16),
        in_specs=[vmem] * 7,
        out_specs=anywhere,
        scratch_shapes=[
            pltpu.VMEM((half_outs, channels), jnp.bfloat16),
            pltpu.VMEM((half_outs, channels), jnp.bfloat16),
            pltpu.VMEM((positions, piles, channels), jnp.bfloat16),
            pltpu.SemaphoreType.DMA((X,)),
        ],
        compiler_params=params,
        cost_estimate=pl.CostEstimate(
            flops=flops, bytes_accessed=4 << 20, transcendentals=count * outputs
        ),
        name="input_grad",
    )(near, far, near_other, far_other, rows, dlogits, flat_head)
    parts, input_grad = lax.optimization_barrier((parts, input_grad))
    copies = pl.pallas_call(
        sum_kernel,
        out_shape=jax.ShapeDtypeStruct((YH * parts.shape[1], deep, shard), jnp.bfloat16),
        in_specs=[vmem],
        out_specs=vmem,
        compiler_params=params,
        name="sum",
    )(parts)
    over_y = jnp.sum(exchange(copies, OVER_Y).astype(jnp.float32), axis=0).astype(jnp.bfloat16)
    parts = exchange(jnp.broadcast_to(over_y, (Z, deep, shard)), OVER_Z)
    mine = jnp.sum(parts.reshape(PAIR, Z // PAIR, deep, shard).astype(jnp.float32), axis=1)
    mine = mine.reshape(half_outs, shard)

    theirs = swap_cores(mine)
    new_weight, new_first, new_second = pl.pallas_call(
        adam_kernel,
        out_shape=(jax.ShapeDtypeStruct((shard, outputs), jnp.float32),) * 3,
        in_specs=[vmem] * 5,
        out_specs=(vmem,) * 3,
        scratch_shapes=[pltpu.VMEM((outputs, shard), jnp.float32)],
        compiler_params=params,
        name="adam",
    )(mine, theirs, weight, moment_one, moment_two)
    return (input_grad.transpose(1, 0, 2), new_weight, new_first, new_second)


def solution(mesh):
    return jax.shard_map(
        per_device,
        mesh=mesh,
        in_specs=(
            P(("dp", "group"), None, None),
            P(("dp", "group")),
            P("group", None),
            P(),
            P("group", None),
            P("group", None),
        ),
        out_specs=(
            P(("dp", "group"), None, None),
            P("group", None),
            P("group", None),
            P("group", None),
        ),
        check_vma=False,
    )
```

```python
import functools
import math

import jax
import jax.numpy as jnp
from jax import lax
from jax.experimental import pallas as pl
from jax.experimental.pallas import tpu as pltpu
from jax.sharding import PartitionSpec as P

beta_one = 0.9
beta_two = 0.999
learn_rate = 0.01
epsilon = 1e-08
bias_steps = 10.0

AXES = ("dp", "group")
Z, YH, CORE, X, YL = 8, 2, 2, 4, 4
GROUP = X * YL
PAIR = 2
root = math.sqrt(2.0 / math.pi)
cubic = 0.044715


def index(z, yh, c, x, yl):
    return ((z * YH + yh) * CORE + c) * GROUP + x * YL + yl


def places():
    for z in range(Z):
        for yh in range(YH):
            for c in range(CORE):
                for x in range(X):
                    for yl in range(YL):
                        yield z, yh, c, x, yl


def groups(key, order):
    held = {}
    for place in places():
        held.setdefault(key(*place), []).append((order(*place), index(*place)))
    return [[at for _, at in sorted(held[name])] for name in sorted(held)]


def pair_of(y, c):
    return (y - 1 + c) % (YH * YL) // PAIR


def beyond(yh, yl, c):
    at = (yh * YL + yl + (-1 if (yl + c) % PAIR else 1)) % (YH * YL)
    return at // YL, at % YL


OVER_XY = groups(
    lambda z, yh, c, x, yl: (z, c, pair_of(yh * YL + yl, c)), lambda z, yh, c, x, yl: (x, yl % PAIR)
)
OVER_XYZ = groups(
    lambda z, yh, c, x, yl: (z // PAIR, yh, c, yl // PAIR), lambda z, yh, c, x, yl: (x, yl % PAIR, z % PAIR)
)
OVER_Y = groups(lambda z, yh, c, x, yl: (z, c, x, yl % PAIR), lambda z, yh, c, x, yl: (yh, yl))
OVER_Z = groups(lambda z, yh, c, x, yl: (yh, c, x, yl), lambda z, yh, c, x, yl: (z % PAIR, z))
SWAP = [(index(z, yh, c, x, yl), index(z, yh, 1 - c, x, yl)) for z, yh, c, x, yl in places()]


CROSS = [
    (index(z, yh, c, x, yl), index(z, beyond(yh, yl, c)[0], c, x, beyond(yh, yl, c)[1]))
    for z, yh, c, x, yl in places()
]


def swap_cores(value):
    return lax.ppermute(value, AXES, SWAP)


def exchange(value, members):
    return lax.all_to_all(value, AXES, 0, 0, tiled=True, axis_index_groups=members)


def core_index():
    return lax.rem(lax.axis_index("dp"), CORE)


def gelu_parts(pre):
    square = pre * pre
    bend = jnp.tanh(root * (pre + cubic * (pre * square)))
    act = 0.5 * pre * (1.0 + bend)
    slope = 0.5 * (1.0 + bend) + 0.5 * pre * (1.0 - bend * bend) * (root * (1.0 + 3.0 * cubic * square))
    return act, slope


def product(rows_ref, weight_ref):
    positions, piles, channels = rows_ref.shape
    return lax.dot_general(
        rows_ref[...].reshape(positions * piles, channels),
        weight_ref[...],
        (((1,), (1,)), ((), ())),
        preferred_element_type=jnp.float32,
    )


def head_half(head_ref, half):
    count = head_ref.shape[1] // 2
    whole = head_ref[...]
    chosen = jnp.where(half == 0, whole[:, :count], whole[:, count:])
    return [chosen[kind : kind + 1, :] for kind in range(head_ref.shape[0])]


def in_lanes(columns):
    lane = lax.broadcasted_iota(jnp.int32, (columns[0].shape[0], 128), 1)
    held = jnp.zeros(lane.shape, jnp.float32)
    for at, column in enumerate(columns):
        held = jnp.where(lane == at, column, held)
    return held


def spread(dlogits, heads, positions):
    dpooled = functools.reduce(jnp.add, [column * vector for column, vector in zip(dlogits, heads)])
    return jnp.concatenate([dpooled / positions] * positions, axis=0)


def prepare_kernel(weight_ref, out_ref, flip_ref):
    half = out_ref.shape[0]
    flip_ref[...] = weight_ref[...].T
    out_ref[...] = flip_ref[pl.ds(pl.multiple_of(core_index() * half, half), half), :].astype(jnp.bfloat16)


def shards_of(core, far):
    yl = lax.rem(lax.axis_index("group"), YL)
    odd = lax.rem(yl, PAIR)
    step = 2 * core - 1
    even_at = lax.rem(yl - odd * step + YL, YL)
    odd_at = lax.rem(yl + (1 - odd) * step + YL, YL)
    return [x * YL + lax.rem(at + PAIR * far, YL) for x in range(X) for at in (even_at, odd_at)]


def assemble(core, near_ref, far_ref, weight_ref):
    width = near_ref.shape[2]
    for far, blocks_ref in enumerate((near_ref, far_ref)):
        for block, shard in enumerate(shards_of(core, far)):
            weight_ref[:, pl.ds(pl.multiple_of(shard * width, width), width)] = blocks_ref[block]


def channels_of(side, span):
    return jnp.concatenate(
        [ref[at, :, span] for ref in side for at in range(ref.shape[0])], axis=0
    )


def partial_product(core, far, blocks_ref, side):
    width = blocks_ref.shape[2]
    shards = shards_of(core, far)
    total = None
    for block in range(0, len(shards), 2):
        spans = [pl.ds(pl.multiple_of(shard * width, width), width) for shard in shards[block : block + 2]]
        part = lax.dot_general(
            jnp.concatenate([channels_of(side, span) for span in spans], axis=1),
            jnp.concatenate([blocks_ref[block], blocks_ref[block + 1]], axis=1),
            (((1,), (1,)), ((), ())),
            preferred_element_type=jnp.float32,
        )
        total = part if total is None else total + part
    return total


def near_kernel(blocks_ref, rows_ref, first_ref, last_ref, pre_ref):
    for at, side in enumerate(((rows_ref,), (first_ref, last_ref))):
        pre_ref[at] = partial_product(core_index(), 0, blocks_ref, side)


def forward_kernel(
    pre_ref, blocks_ref, rows_ref, first_ref, last_ref, labels_ref, head_ref, slope_ref, logits_ref
):
    positions, piles, channels = rows_ref.shape
    heads = head_half(head_ref, core_index())
    across = lax.broadcasted_iota(jnp.int32, (piles, piles), 0) == lax.broadcasted_iota(
        jnp.int32, (piles, piles), 1
    )
    marks = jnp.sum(
        jnp.where(across, labels_ref[...].astype(jnp.float32), 0.0), axis=1, keepdims=True
    )
    for side, refs in enumerate(((rows_ref,), (first_ref, last_ref))):
        pre = pre_ref[side] + partial_product(core_index(), 1, blocks_ref, refs)
        act, slope = gelu_parts(pre)
        slope_ref[side] = slope
        pooled = functools.reduce(
            jnp.add, [act[position * piles : (position + 1) * piles] for position in range(positions)]
        )
        pooled = pooled / positions
        logits = [jnp.sum(pooled * vector, axis=1, keepdims=True) for vector in heads]
        logits_ref[side] = in_lanes(logits + [marks] if side == 0 else logits)


def gradient_kernel(
    logits_ref, received_ref, slope_ref, rows_ref, first_ref, last_ref, head_ref, grad_ref, dlogits_ref
):
    positions, piles, channels = rows_ref.shape
    classes = head_ref.shape[0]
    heads = head_half(head_ref, core_index())
    lefts = []
    for side in range(CORE):
        mine, theirs = logits_ref[side], received_ref[1 - side]
        marks = (mine if side == 0 else theirs)[:, classes : classes + 1]
        logits = [mine[:, kind : kind + 1] + theirs[:, kind : kind + 1] for kind in range(classes)]
        top = functools.reduce(jnp.maximum, logits)
        powers = [jnp.exp(value - top) for value in logits]
        total = functools.reduce(jnp.add, powers)
        dlogits = [
            powers[kind] / total - jnp.where(marks == float(kind), 1.0, 0.0) for kind in range(classes)
        ]
        dpre = spread(dlogits, heads, positions) * slope_ref[side]
        if side == 0:
            dlogits_ref[...] = in_lanes(dlogits)
        lefts.append(dpre.T.astype(jnp.bfloat16))
    wide = channels // X
    width = wide // YL
    deep = lefts[0].shape[0] // PAIR
    for x in range(X):
        parts = [
            jnp.dot(
                left,
                channels_of(refs, slice(x * wide, (x + 1) * wide)),
                preferred_element_type=jnp.float32,
            )
            for left, refs in zip(lefts, ((rows_ref,), (first_ref, last_ref)))
        ]
        total = (parts[0] + parts[1]).astype(jnp.bfloat16)
        for part in range(PAIR):
            for yl in range(YL):
                grad_ref[x, yl % PAIR, part, yl // PAIR] = total[
                    part * deep : (part + 1) * deep, yl * width : (yl + 1) * width
                ]


def sum_kernel(parts_ref, out_ref):
    count, rows = parts_ref.shape[:2]
    total = parts_ref[0].astype(jnp.float32)
    for at in range(1, count):
        total = total + parts_ref[at].astype(jnp.float32)
    for copy in range(out_ref.shape[0] // rows):
        out_ref[copy * rows : (copy + 1) * rows] = total.astype(jnp.bfloat16)


def input_kernel(
    near_ref, far_ref, near_other_ref, far_other_ref, rows_ref, dlogits_ref, head_ref, input_ref,
    weight_ref, other_ref, held_ref, sems
):
    positions, piles, channels = rows_ref.shape
    assemble(core_index(), near_ref, far_ref, weight_ref)
    assemble(1 - core_index(), near_other_ref, far_other_ref, other_ref)
    dlogits = [dlogits_ref[:, kind : kind + 1] for kind in range(head_ref.shape[0])]
    dpres = []
    for half, half_ref in ((core_index(), weight_ref), (1 - core_index(), other_ref)):
        slope = gelu_parts(product(rows_ref, half_ref))[1]
        dpres.append((spread(dlogits, head_half(head_ref, half), positions) * slope).astype(jnp.bfloat16))
    wide = channels // X
    copies = []
    for x in range(X):
        span = pl.ds(x * wide, wide)
        back = jnp.dot(dpres[0], weight_ref[:, span], preferred_element_type=jnp.float32)
        back = back + jnp.dot(dpres[1], other_ref[:, span], preferred_element_type=jnp.float32)
        held_ref[:, :, span] = back.astype(jnp.bfloat16).reshape(positions, piles, wide)
        copies.append(
            pltpu.make_async_copy(held_ref.at[:, :, span], input_ref.at[:, :, span], sems.at[x])
        )
        copies[-1].start()
    for copy in copies:
        copy.wait()


def adam_kernel(
    own_ref, other_ref, weight_ref, first_ref, second_ref, out_weight, out_first, out_second, flip_ref, held_ref, sems
):
    half = own_ref.shape[0]
    core = core_index()
    copies = []

    def send(at, value, out_ref):
        held_ref[at] = value
        copies.append(pltpu.make_async_copy(held_ref.at[at], out_ref, sems.at[at]))
        copies[-1].start()

    flip_ref[pl.ds(pl.multiple_of(core * half, half), half), :] = own_ref[...]
    flip_ref[pl.ds(pl.multiple_of((1 - core) * half, half), half), :] = other_ref[...]
    grad = flip_ref[...].T
    new_first = beta_one * first_ref[...] + (1.0 - beta_one) * grad
    send(0, new_first, out_first)
    new_second = beta_two * second_ref[...] + (1.0 - beta_two) * grad * grad
    send(1, new_second, out_second)
    first_hat = new_first / (1.0 - beta_one**bias_steps)
    second_hat = new_second / (1.0 - beta_two**bias_steps)
    send(2, weight_ref[...] - learn_rate * first_hat / (jnp.sqrt(second_hat) + epsilon), out_weight)
    for copy in copies:
        copy.wait()


def per_device(features, labels, weight, head, moment_one, moment_two):
    piles, positions, channels = features.shape
    shard, outputs = weight.shape
    count = piles * positions
    half_outs = outputs // 2
    deep = half_outs // PAIR
    rows = features.transpose(1, 0, 2)
    flat_head = head.T
    vmem = pl.BlockSpec(memory_space=pltpu.VMEM)
    anywhere = pl.BlockSpec(memory_space=pl.ANY)
    params = pltpu.CompilerParams(vmem_limit_bytes=16 << 20)

    half = pl.pallas_call(
        prepare_kernel,
        out_shape=jax.ShapeDtypeStruct((half_outs, shard), jnp.bfloat16),
        in_specs=[vmem],
        out_specs=vmem,
        scratch_shapes=[pltpu.VMEM((outputs, shard), jnp.float32)],
        compiler_params=params,
        name="prepare",
    )(weight)
    sent_rows, half = lax.optimization_barrier((rows, half))
    near = exchange(jnp.broadcast_to(half, (X * PAIR, half_outs, shard)), OVER_XY)
    later_rows, near = lax.optimization_barrier((rows, near))
    other_rows = (swap_cores(sent_rows[:4]), swap_cores(later_rows[4:]))
    far = lax.ppermute(near, AXES, CROSS)

    flops = 2 * count * channels * outputs
    pre = pl.pallas_call(
        near_kernel,
        out_shape=jax.ShapeDtypeStruct((CORE, count, half_outs), jnp.float32),
        in_specs=[vmem] * 4,
        out_specs=vmem,
        compiler_params=params,
        cost_estimate=pl.CostEstimate(flops=flops // 2, bytes_accessed=4 << 20, transcendentals=0),
        name="forward_near",
    )(near, rows, *other_rows)
    slope, logits = pl.pallas_call(
        forward_kernel,
        out_shape=(
            jax.ShapeDtypeStruct((CORE, count, half_outs), jnp.float32),
            jax.ShapeDtypeStruct((CORE, piles, 128), jnp.float32),
        ),
        in_specs=[vmem] * 7,
        out_specs=(vmem,) * 2,
        compiler_params=params,
        cost_estimate=pl.CostEstimate(
            flops=flops // 2, bytes_accessed=4 << 20, transcendentals=count * outputs
        ),
        name="forward_far",
    )(pre, far, rows, *other_rows, labels.reshape(1, piles), flat_head)

    received = swap_cores(logits)
    grad, dlogits = pl.pallas_call(
        gradient_kernel,
        out_shape=(
            jax.ShapeDtypeStruct((X, PAIR, PAIR, YL // PAIR, deep, shard), jnp.bfloat16),
            jax.ShapeDtypeStruct((piles, 128), jnp.float32),
        ),
        in_specs=[vmem] * 7,
        out_specs=(vmem,) * 2,
        compiler_params=params,
        cost_estimate=pl.CostEstimate(flops=flops, bytes_accessed=4 << 20, transcendentals=0),
        name="gradient",
    )(logits, received, slope, rows, *other_rows, flat_head)

    both = grad.reshape(GROUP, -1, deep, shard)
    parts = exchange(both, OVER_XYZ)
    near_other, far_other = swap_cores(near), swap_cores(far)
    input_grad = pl.pallas_call(
        input_kernel,
        out_shape=jax.ShapeDtypeStruct((positions, piles, channels), jnp.bfloat16),
        in_specs=[vmem] * 7,
        out_specs=anywhere,
        scratch_shapes=[
            pltpu.VMEM((half_outs, channels), jnp.bfloat16),
            pltpu.VMEM((half_outs, channels), jnp.bfloat16),
            pltpu.VMEM((positions, piles, channels), jnp.bfloat16),
            pltpu.SemaphoreType.DMA((X,)),
        ],
        compiler_params=params,
        cost_estimate=pl.CostEstimate(
            flops=flops, bytes_accessed=4 << 20, transcendentals=count * outputs
        ),
        name="input_grad",
    )(near, far, near_other, far_other, rows, dlogits, flat_head)
    parts, input_grad = lax.optimization_barrier((parts, input_grad))
    copies = pl.pallas_call(
        sum_kernel,
        out_shape=jax.ShapeDtypeStruct((YH * parts.shape[1], deep, shard), jnp.bfloat16),
        in_specs=[vmem],
        out_specs=vmem,
        compiler_params=params,
        name="sum",
    )(parts)
    copies = pl.pallas_call(
        sum_kernel,
        out_shape=jax.ShapeDtypeStruct((Z, deep, shard), jnp.bfloat16),
        in_specs=[vmem],
        out_specs=vmem,
        compiler_params=params,
        name="sum_y",
    )(exchange(copies, OVER_Y).reshape(-1, 1, deep, shard))
    parts = exchange(copies, OVER_Z)
    mine = jnp.sum(parts.reshape(PAIR, Z // PAIR, deep, shard).astype(jnp.float32), axis=1)
    mine = mine.reshape(half_outs, shard)

    theirs = swap_cores(mine)
    new_weight, new_first, new_second = pl.pallas_call(
        adam_kernel,
        out_shape=(jax.ShapeDtypeStruct((shard, outputs), jnp.float32),) * 3,
        in_specs=[vmem] * 5,
        out_specs=(anywhere,) * 3,
        scratch_shapes=[
            pltpu.VMEM((outputs, shard), jnp.float32),
            pltpu.VMEM((3, shard, outputs), jnp.float32),
            pltpu.SemaphoreType.DMA((3,)),
        ],
        compiler_params=params,
        name="adam",
    )(mine, theirs, weight, moment_one, moment_two)
    return (input_grad.transpose(1, 0, 2), new_weight, new_first, new_second)


def solution(mesh):
    return jax.shard_map(
        per_device,
        mesh=mesh,
        in_specs=(
            P(("dp", "group"), None, None),
            P(("dp", "group")),
            P("group", None),
            P(),
            P("group", None),
            P("group", None),
        ),
        out_specs=(
            P(("dp", "group"), None, None),
            P("group", None),
            P("group", None),
            P("group", None),
        ),
        check_vma=False,
    )
```
